512 devices in a mesh: section: 2 (over core), tile: 32 (over z, x_lo), set: 8 (over y, x_hi).
Axes of the slice: x: 4 (x_hi: 2, x_lo: 2; x = x_hi * 2 + x_lo), y: 4, z: 16, core: 2. Of those that a mesh axis runs over, the one named last changes fastest.
Arguments:
- features: bfloat16 [16, 96, 128, 384], P('set', 'tile', 'section'), may hold values from -6 to 6
- tissue: int32 [16, 96, 128], P('set', 'tile', 'section'), may hold values from 0 to 1, as said below
- partner: int32 [16], replicated, may hold values from 0 to 15, as said below
- dw_kernel: float32 [7, 7, 384], replicated, may hold values from -0.875 to 0.875
- dw_bias: float32 [384], replicated, may hold values from -3 to 3
- ln_gain: float32 [384], replicated, may hold values from 0.5 to 1.5
- ln_bias: float32 [384], replicated, may hold values from -2 to 2
- w_up: bfloat16 [384, 1536], replicated, may hold values from -0.3125 to 0.3125
- narrowing_projection_kernel: bfloat16 [1536, 384], replicated, may hold values from -0.15625 to 0.15625
- layer_scale: float32 [384], replicated, may hold values from 0.2 to 1
- w_embed: bfloat16 [384, 1024], replicated, may hold values from -0.3125 to 0.3125
- embed_bias: float32 [1024], replicated, may hold values from -3 to 3
- attn_v: bfloat16 [1024, 256], replicated, may hold values from -0.1875 to 0.1875
- attn_u: bfloat16 [1024, 256], replicated, may hold values from -0.1875 to 0.1875
- attn_w: float32 [256], replicated, may hold values from -0.2 to 0.2
Outputs:
- slide_loss: float32 [16], P('set')
- specimen_normalised_vector: float32 [16, 1024], P('set')
- boundary_grad: bfloat16 [16, 96, 128, 384], P('set', 'tile', 'section')
The draws below stay inside these ranges and needn't reach their ends.
Inputs may be any that keep to these rules, and one draw needn't show every extreme that they name: Every slide has at least one tissue tile. Slides come in positive pairs: partner[partner[s]] = s and partner[s] != s.
All inputs are finite; a program needn't handle non-finite values.
Results may differ from the reference program's by a relative error of at most 0.0118.
Values may be sent and summed in bfloat16 or wider, within the bound.
No kernel may reach another device: no remote copies, remote signals or barrier semaphores. Data moves between devices by JAX's collectives and lax.ppermute only.
A program may use at most 64 MiB of HBM per device.

```python
import math
from functools import partial
import jax
import jax.numpy as jnp
from jax import lax

C = 384
HID = 1536
A = 1024
AH = 256
SLIDES = 16
GH = 96
GW = 128


def draw_tissue(key, part):
    key = jax.random.fold_in(key, 11)
    keys_list = jax.random.split(key, 5)
    shape_one = (SLIDES, 1, 1)
    centre_row = jax.random.randint(keys_list[0], shape_one, 0, GH)
    centre_col = jax.random.randint(keys_list[1], shape_one, 0, GW)
    radius_row = jax.random.randint(keys_list[2], shape_one, max(GH // 8, 1), max(GH // 2, 2))
    radius_col = jax.random.randint(keys_list[3], shape_one, max(GW // 8, 1), max(GW // 2, 2))
    row_index = jnp.arange(GH, dtype=jnp.int32)[None, :, None]
    col_index = jnp.arange(GW, dtype=jnp.int32)[None, None, :]
    row_step = (row_index - centre_row) * 16 // radius_row
    col_step = (col_index - centre_col) * 16 // radius_col
    inside = row_step * row_step + col_step * col_step <= 256
    intact = jax.random.randint(keys_list[4], (SLIDES, GH, GW), 0, 8) != 0
    centre = (row_index == centre_row) & (col_index == centre_col)
    return (inside & intact | centre).astype(jnp.int32)


def draw_partner(key, part):
    key = jax.random.fold_in(key, 23)
    raw_scores = jax.random.randint(key, (SLIDES,), 0, 1 << 20, dtype=jnp.int32)
    distinct = raw_scores * SLIDES + jnp.arange(SLIDES, dtype=jnp.int32)
    ordering = jnp.argsort(distinct, stable=True).astype(jnp.int32)
    position = jnp.argsort(ordering, stable=True).astype(jnp.int32)
    mate_position = jnp.bitwise_xor(position, 1)
    return ordering[mate_position].astype(jnp.int32)


def block_levels(stream_key, extent, cuts, smallest, high):
    def one(dim, blocks):
        draws = jax.random.uniform(jax.random.fold_in(jax.random.fold_in(stream_key, 6), dim), (blocks,), jnp.float32, smallest / len(cuts), high / len(cuts))
        return jnp.repeat(jnp.exp(draws), extent[dim] // blocks).reshape((-1,) + (1,) * (len(extent) - dim - 1))

    loudness = one(*cuts[0])
    for cut in cuts[1:]:
        loudness = loudness * one(*cut)
    return loudness


def bell_draw(own_key, shape, spread, most, cuts=(), kind=jnp.bfloat16):
    factor_of = block_levels(own_key, shape, cuts, -0.22, 0.18) if cuts else 1.0
    values = jax.random.normal(own_key, shape, jnp.float32) * spread * factor_of
    return jnp.minimum(jnp.maximum(values, -most), most).astype(kind)


def setup_inputs(seed: int = 0) -> dict:
    seeds = jax.random.split(jax.random.key(seed), 16)
    features = bell_draw(seeds[0], (SLIDES, GH, GW, C), 1.0, 6.0, ((0, 8), (1, 32), (2, 2)))
    tissue = draw_tissue(jax.random.fold_in(seeds[15], 71), 0)
    partner = draw_partner(jax.random.fold_in(seeds[15], 71), 0)
    dw_kernel = bell_draw(seeds[3], (7, 7, C), 49 ** -0.5, 0.875, (), jnp.float32)
    dw_bias = bell_draw(seeds[4], (C,), 0.5, 3.0, (), jnp.float32)
    ln_gain = jnp.clip(1.0 + 0.1 * jax.random.normal(seeds[5], (C,), jnp.float32), 0.5, 1.5)
    ln_bias = bell_draw(seeds[6], (C,), 0.3, 2.0, (), jnp.float32)
    w_up = bell_draw(seeds[7], (C, HID), C ** -0.5, 0.3125)
    narrowing_projection_kernel = bell_draw(seeds[8], (HID, C), HID ** -0.5, 0.15625)
    layer_scale = jnp.clip(jnp.exp(jax.random.uniform(seeds[9], (C,), jnp.float32, math.log(0.2), math.log(1.0))), 0.2, 1.0)
    w_embed = bell_draw(seeds[10], (C, A), C ** -0.5, 0.3125)
    embed_bias = bell_draw(seeds[11], (A,), 0.5, 3.0, (), jnp.float32)
    attn_v = bell_draw(seeds[12], (A, AH), A ** -0.5, 0.1875)
    attn_u = bell_draw(seeds[13], (A, AH), A ** -0.5, 0.1875)
    attn_w = jnp.clip(jax.random.uniform(seeds[14], (AH,), jnp.float32, -0.2, 0.2), -0.2, 0.2)
    return {"features": features, "tissue": tissue, "partner": partner, "dw_kernel": dw_kernel, "dw_bias": dw_bias, "ln_gain": ln_gain, "ln_bias": ln_bias, "w_up": w_up, "narrowing_projection_kernel": narrowing_projection_kernel, "layer_scale": layer_scale, "w_embed": w_embed, "embed_bias": embed_bias, "attn_v": attn_v, "attn_u": attn_u, "attn_w": attn_w}


logit_sharpness_divisor = 0.1
loss_scale = 65536.0
finest_accuracy_mode = lax.Precision.HIGHEST

def depthwise(padded, dw_kernel, dw_bias, out_rows, out_cols):
    result = jnp.zeros(padded.shape[:-3] + (out_rows, out_cols, padded.shape[-1]), jnp.float32)
    for offset_row in range(7):
        for offset_col in range(7):
            window = lax.slice_in_dim(padded, offset_row, offset_row + out_rows, axis=padded.ndim - 3)
            window = lax.slice_in_dim(window, offset_col, offset_col + out_cols, axis=padded.ndim - 2)
            result = result + window.astype(jnp.float32) * dw_kernel[offset_row, offset_col]
    return result + dw_bias

def pointwise(convolved, masked, weight_grid, ln_gain, ln_bias, w_up, narrowing_projection_kernel, layer_scale):
    centre = lax.optimization_barrier(jnp.mean(convolved, axis=-1, keepdims=True))
    spread_sq = lax.optimization_barrier(jnp.mean(jnp.square(convolved - centre), axis=-1, keepdims=True))
    normed = ((convolved - centre) * lax.rsqrt(spread_sq + 1e-06) * ln_gain + ln_bias).astype(jnp.bfloat16)
    flattened = normed.reshape(-1, normed.shape[-1])
    hidden = jax.nn.gelu(jnp.dot(flattened, w_up, preferred_element_type=jnp.float32), approximate=False).astype(jnp.bfloat16)
    branch = jnp.dot(hidden, narrowing_projection_kernel, preferred_element_type=jnp.float32).reshape(convolved.shape)
    return ((masked.astype(jnp.float32) + layer_scale * branch) * weight_grid[..., None]).astype(jnp.bfloat16)

def embed_rows(tile_rows, w_embed, embed_bias, attn_v, attn_u, attn_w):
    pre_act = jnp.dot(tile_rows, w_embed, preferred_element_type=jnp.float32) + embed_bias
    embedded = jax.nn.gelu(pre_act, approximate=False).astype(jnp.bfloat16)
    tangent = jnp.tanh(jnp.dot(embedded, attn_v, preferred_element_type=jnp.float32))
    opening = jax.nn.sigmoid(jnp.dot(embedded, attn_u, preferred_element_type=jnp.float32))
    scores = lax.optimization_barrier(jnp.sum(tangent * opening * attn_w, axis=-1))
    return (pre_act, embedded, tangent, opening, scores)

def back_rows(pre_act, embedded, tangent, opening, shares, grad_rows, grad_dot, w_embed, attn_v, attn_u, attn_w):
    score_grad = shares * (lax.optimization_barrier(jnp.sum(grad_rows * embedded.astype(jnp.float32), axis=-1)) - grad_dot)
    grad_tan = (score_grad[:, None] * attn_w * opening * (1.0 - tangent * tangent)).astype(jnp.bfloat16)
    grad_open = (score_grad[:, None] * attn_w * tangent * opening * (1.0 - opening)).astype(jnp.bfloat16)
    contract = (((1,), (1,)), ((), ()))
    feature_vector_derivative = shares[:, None] * grad_rows
    feature_vector_derivative = feature_vector_derivative + lax.dot_general(grad_tan, attn_v, contract, preferred_element_type=jnp.float32)
    feature_vector_derivative = feature_vector_derivative + lax.dot_general(grad_open, attn_u, contract, preferred_element_type=jnp.float32)
    pre_grad = jax.vjp(partial(jax.nn.gelu, approximate=False), pre_act)[1](feature_vector_derivative)[0].astype(jnp.bfloat16)
    return lax.dot_general(pre_grad, w_embed, contract, preferred_element_type=jnp.float32).astype(jnp.bfloat16)

def contrast_rows(cosine_score_table, row_ids, partner_rows):
    columns = jnp.arange(cosine_score_table.shape[1], dtype=jnp.int32)
    others = columns[None, :] != row_ids[:, None]
    exp_sims = jnp.where(others, jnp.exp(cosine_score_table), 0.0)
    normaliser = lax.optimization_barrier(jnp.sum(exp_sims, axis=-1))
    positive = (columns[None, :] == partner_rows[:, None]).astype(jnp.float32)
    losses = jnp.log(normaliser) - lax.optimization_barrier(jnp.sum(positive * cosine_score_table, axis=-1))
    contrastive_probability_table = exp_sims / normaliser[:, None] - positive
    return (losses, contrastive_probability_table)

def normalise(weighted_sum, totals):
    pooled = weighted_sum / totals[:, None]
    radius = jnp.sqrt(lax.optimization_barrier(jnp.sum(pooled * pooled, axis=-1)) + 1e-06)
    return (pooled, radius, pooled / radius[:, None])

def pooled_gradient(pooled, radius, feature_vector_derivative):
    projection = lax.optimization_barrier(jnp.sum(pooled * feature_vector_derivative, axis=-1))
    return loss_scale * (feature_vector_derivative / radius[:, None] - pooled * (projection / (radius * radius * radius))[:, None])

def reference(features, tissue, partner, dw_kernel, dw_bias, ln_gain, ln_bias, w_up, narrowing_projection_kernel, layer_scale, w_embed, embed_bias, attn_v, attn_u, attn_w):

    def trunk_slide(slide_pair):
        slide_feats, slide_flags = slide_pair
        masked = slide_feats * slide_flags.astype(jnp.bfloat16)[..., None]
        padded = jnp.pad(masked, ((3, 3), (3, 3), (0, 0)))
        convolved = depthwise(padded, dw_kernel, dw_bias, GH, GW)
        return pointwise(convolved, masked, slide_flags.astype(jnp.float32), ln_gain, ln_bias, w_up, narrowing_projection_kernel, layer_scale)
    trunk_out = lax.map(trunk_slide, (features, tissue))

    def forward_slide(slide_pair):
        slide_out, slide_flags = slide_pair
        pre_act, embedded, tangent, opening, scores = embed_rows(slide_out.reshape(-1, C), w_embed, embed_bias, attn_v, attn_u, attn_w)
        learned_parameters = slide_flags.reshape(-1).astype(jnp.float32) * jnp.exp(scores)
        return (lax.optimization_barrier(jnp.sum(learned_parameters[:, None] * embedded.astype(jnp.float32), axis=0)), jnp.sum(learned_parameters))
    weighted_sum, totals = lax.map(forward_slide, (trunk_out, tissue))
    pooled, radius, specimen_normalised_vector = normalise(weighted_sum, totals)
    cosine_score_table = jnp.dot(specimen_normalised_vector, specimen_normalised_vector.T, precision=finest_accuracy_mode) / logit_sharpness_divisor
    slide_loss, contrastive_probability_table = contrast_rows(cosine_score_table, jnp.arange(SLIDES, dtype=jnp.int32), partner)
    feature_vector_derivative = (jnp.dot(contrastive_probability_table, specimen_normalised_vector, precision=finest_accuracy_mode) + jnp.dot(contrastive_probability_table.T, specimen_normalised_vector, precision=finest_accuracy_mode)) / logit_sharpness_divisor
    pooled_grad = pooled_gradient(pooled, radius, feature_vector_derivative)
    grad_dots = lax.optimization_barrier(jnp.sum(pooled_grad * pooled, axis=-1))

    def backward_slide(slide_pair):
        slide_out, slide_flags, slide_grad, slide_dot, slide_total = slide_pair
        pre_act, embedded, tangent, opening, scores = embed_rows(slide_out.reshape(-1, C), w_embed, embed_bias, attn_v, attn_u, attn_w)
        shares = slide_flags.reshape(-1).astype(jnp.float32) * jnp.exp(scores) / slide_total
        tile_count = shares.shape[0]
        grad_rows = jnp.broadcast_to(slide_grad[None, :], (tile_count, slide_grad.shape[0]))
        grad_dot = jnp.broadcast_to(slide_dot, (tile_count,))
        fresh = back_rows(pre_act, embedded, tangent, opening, shares, grad_rows, grad_dot, w_embed, attn_v, attn_u, attn_w)
        return fresh.reshape(GH, GW, C)
    boundary_grad = lax.map(backward_slide, (trunk_out, tissue, pooled_grad, grad_dots, totals))
    return (slide_loss, specimen_normalised_vector, boundary_grad)
```

```python
import jax
import jax.numpy as jnp
from jax import lax
from jax.experimental import pallas as pl
from jax.experimental.pallas import tpu as pltpu
from jax.sharding import Mesh
from jax.sharding import PartitionSpec as P

C = 384
HID = 1536
A = 1024
AH = 256
S = 2
R = 3
W = 64
N = S * R * W
PW = W + 8
LANES = 128
HALF = S * R * W // S
INV_T = 10.0
SCALE = 65536.0
RSQRT2 = 0.7071067811865476
RSQRT2PI = 0.3989422804014327
NT = (((1,), (1,)), ((), ()))
HI = lax.Precision.HIGHEST
F32 = jnp.float32
BF = jnp.bfloat16


def copies_between(pairs, sems, first=0):
    return [
        pltpu.make_async_copy(src, dst, sems.at[first + i]) for i, (src, dst) in enumerate(pairs)
    ]


def mask_kernel(
    features_hbm, tissue, masked_hbm, edge_hbm, flags_hbm, features, masked, edge, flags, sems
):
    where = [(s, r) for s in range(S) for r in range(R)]
    arrive = copies_between([(features_hbm.at[p], features.at[p]) for p in where], sems)
    leave = copies_between([(masked.at[p], masked_hbm.at[p]) for p in where], sems, S * R)
    last_out = copies_between([(edge, edge_hbm), (flags, flags_hbm)], sems, 2 * S * R)
    for c in arrive:
        c.start()
    side = lax.axis_index("section")
    place = lax.broadcasted_iota(jnp.int32, (8, C), 0)
    first = jnp.where((place < 3) & (side == 1), 1.0, 0.0)
    last = jnp.where((place >= 5) & (side == 0), 1.0, 0.0)
    for i, (s, r) in enumerate(where):
        row = tissue[r, s : s + 1, :].astype(F32)
        here = jnp.broadcast_to(row, (LANES, W)).T
        flags[i * W : i * W + W, :] = here
        wide = jnp.concatenate([here] * (C // LANES), axis=1)
        arrive[i].wait()
        values = features[s, r].astype(F32) * wide
        masked[s, r] = values.astype(BF)
        leave[i].start()
        edge[s, r] = (values[:8] * first + values[W - 8 :] * last).astype(BF)
    for c in last_out:
        c.start()
    for c in leave + last_out:
        c.wait()


def forward_kernel(
    own_hbm, above_hbm, below_hbm, edge_own_hbm, edge_above_hbm, edge_below_hbm, flags_hbm,
    dw_k_hbm, dw_b_hbm, ln_g_hbm, ln_b_hbm, scale_hbm, e_bias_hbm, a_w_hbm,
    up_hbm, down_hbm, emb_hbm, v_hbm, u_hbm,
    payload_hbm, embedded_hbm, slope_hbm, weight_hbm, gate_v_hbm, gate_u_hbm,
    own, above, below, edge_own, edge_above, edge_below, flags,
    dw_k, dw_b, ln_g, ln_b, scale, e_bias, a_w, up, down, emb, att_v, att_u,
    payload, embedded_out, slope_out, weight_out, gate_v_out, gate_u_out,
    grid_ref, acc_ref, conv_ref, sums_ref, sems,
):
    blocks = copies_between(
        (
            (own_hbm, own), (edge_own_hbm, edge_own), (above_hbm, above),
            (edge_above_hbm, edge_above), (below_hbm, below), (edge_below_hbm, edge_below),
        ),
        sems,
    )
    small = copies_between(
        (
            (dw_k_hbm, dw_k), (dw_b_hbm, dw_b), (ln_g_hbm, ln_g), (ln_b_hbm, ln_b),
            (scale_hbm, scale), (e_bias_hbm, e_bias), (a_w_hbm, a_w), (flags_hbm, flags),
        ),
        sems,
        6,
    )
    copies = copies_between(
        ((up_hbm, up), (down_hbm, down), (emb_hbm, emb), (v_hbm, att_v), (u_hbm, att_u)), sems, 14
    )
    results = copies_between(
        (
            (embedded_out, embedded_hbm), (slope_out, slope_hbm), (payload, payload_hbm),
            (weight_out, weight_hbm), (gate_v_out, gate_v_hbm), (gate_u_out, gate_u_hbm),
        ),
        sems,
        19,
    )
    for c in blocks + small + copies:
        c.start()
    for c in blocks + small:
        c.wait()
    for s in range(S):
        for r in range(R):
            for base, (block, edge) in enumerate(
                ((above, edge_above), (own, edge_own), (below, edge_below))
            ):
                grid_ref[s, base * R + r, 0:W, :] = block[s, r].astype(F32)
                grid_ref[s, base * R + r, W:PW, :] = edge[s, r].astype(F32)

    def conv_lane(step, carry):
        s = step // (C // LANES)
        lane = pl.multiple_of(lax.rem(step, C // LANES) * LANES, LANES)
        for col in range(PW // 8):
            cols = slice(col * 8, col * 8 + 8)
            rows = [grid_ref[s, r, cols, pl.ds(lane, LANES)] for r in range(3 * R)]
            for b in range(7):
                sums = [None] * R
                for a in range(7):
                    k = dw_k[a, b, pl.ds(lane, LANES)].reshape(1, LANES)
                    for i in range(R):
                        term = rows[i + a] * k
                        sums[i] = term if sums[i] is None else sums[i] + term
                for i in range(R):
                    acc_ref[i, b, cols, :] = sums[i]
        for i in range(R):
            total = acc_ref[i, 3]
            for b in (0, 1, 2, 4, 5, 6):
                total = total + pltpu.roll(acc_ref[i, b], (3 - b) % PW, 0)
            at = pl.multiple_of(s * R * W + i * W, W)
            conv_ref[pl.ds(at, W), pl.ds(lane, LANES)] = total[0:W]
        return carry

    lax.fori_loop(0, S * (C // LANES), conv_lane, 0)
    conv = conv_ref[...] + dw_b[...].reshape(1, -1)
    centre = jnp.mean(conv, axis=-1, keepdims=True)
    moved = conv - centre
    spread = jnp.mean(moved * moved, axis=-1, keepdims=True)
    normed = (moved * lax.rsqrt(spread + 1e-06) * ln_g[...].reshape(1, -1) + ln_b[...].reshape(1, -1)).astype(BF)
    copies[0].wait()
    copies[1].wait()
    branch = jnp.zeros((N, C), F32)
    step = 384
    for h in range(0, HID, step):
        raised = jnp.dot(normed, up[:, h : h + step], preferred_element_type=F32)
        hidden = (0.5 * raised * (1.0 + lax.erf(raised * RSQRT2))).astype(BF)
        branch = branch + jnp.dot(hidden, down[h : h + step, :], preferred_element_type=F32)
    tissue = flags[...]
    wide = jnp.concatenate([tissue] * (C // LANES), axis=1)
    masked = own[...].reshape(N, C).astype(F32)
    trunk = ((masked + scale[...].reshape(1, -1) * branch) * wide).astype(BF)
    copies[2].wait()
    copies[3].wait()
    copies[4].wait()
    logits_v = jnp.zeros((N, AH), F32)
    logits_u = jnp.zeros((N, AH), F32)
    step = 256
    for h in range(0, A, step):
        cols = slice(h, h + step)
        pre = jnp.dot(trunk, emb[:, cols], preferred_element_type=F32) + e_bias[cols].reshape(1, -1)
        cdf = 0.5 * (1.0 + lax.erf(pre * RSQRT2))
        slope = cdf + pre * (RSQRT2PI * jnp.exp(-0.5 * pre * pre))
        out = (pre * cdf).astype(BF)
        embedded_out[:, cols] = out
        slope_out[:, cols] = slope.astype(BF)
        logits_v = logits_v + jnp.dot(out, att_v[cols, :], preferred_element_type=F32)
        logits_u = logits_u + jnp.dot(out, att_u[cols, :], preferred_element_type=F32)
    results[0].start()
    results[1].start()
    tangent = jnp.tanh(logits_v)
    opening = jax.nn.sigmoid(logits_u)
    aw = a_w[...].reshape(1, -1)
    product = tangent * opening * aw
    scores = jnp.sum(product, axis=-1, keepdims=True)
    weight = tissue * jnp.exp(scores)
    weight_out[...] = weight
    results[3].start()
    for s in range(S):
        rows = slice(s * HALF, s * HALF + HALF)
        w_here = weight[rows, :]
        for k in range(A // LANES):
            cols = slice(k * LANES, k * LANES + LANES)
            part = jnp.sum(w_here * embedded_out[rows, cols].astype(F32), axis=0, keepdims=True)
            sums_ref[s : s + 1, cols] = part
        sums_ref[s : s + 1, A:] = jnp.sum(w_here, axis=0, keepdims=True)
    payload[...] = jnp.broadcast_to(sums_ref[...][None], payload.shape)
    results[2].start()
    gate_v_out[...] = (aw * opening * (1.0 - tangent * tangent)).astype(BF)
    gate_u_out[...] = (product * (1.0 - opening)).astype(BF)
    results[4].start()
    results[5].start()
    for c in results:
        c.wait()


def slope_kernel(
    gate_v, gate_u, slope, emb_hbm, v_hbm, u_hbm, out, emb, att_v, att_u, sems
):
    copies = [
        pltpu.make_async_copy(src, dst, sems.at[i])
        for i, (src, dst) in enumerate(((v_hbm, att_v), (u_hbm, att_u), (emb_hbm, emb)))
    ]
    for c in copies:
        c.start()
    for c in copies:
        c.wait()
    total = jnp.zeros((N, C), F32)
    step = 256
    for h in range(0, A, step):
        cols = slice(h, h + step)
        back = lax.dot_general(gate_v[...], att_v[cols, :], NT, preferred_element_type=F32)
        back = back + lax.dot_general(gate_u[...], att_u[cols, :], NT, preferred_element_type=F32)
        back = (back * slope[:, cols].astype(F32)).astype(BF)
        total = total + lax.dot_general(back, emb[:, cols], NT, preferred_element_type=F32)
    out[...] = total


def sum_kernel(received, ahead, payload):
    total = jnp.sum(received[...], axis=0)
    payload[...] = jnp.broadcast_to(total[None], payload.shape)


def final_kernel(
    received, partner, embedded, slope, weight, gate_term, emb_hbm,
    loss_out, vector_out, grad_out, sums_ref, emb, sem,
):
    fetch = pltpu.make_async_copy(emb_hbm, emb, sem)
    fetch.start()
    position = lax.axis_index("set")
    slides = sums_ref.shape[0]
    groups = slides // S
    for g in range(groups):
        gathered = received[g]
        for part in range(1, received.shape[0] // groups):
            gathered = gathered + received[part * groups + g]
        sums_ref[g * S : g * S + S, :] = gathered
    totals = sums_ref[:, A:]
    pooled = sums_ref[:, :A] / totals[:, :1]
    radius = jnp.sqrt(jnp.sum(pooled * pooled, axis=-1, keepdims=True) + 1e-06)
    vector = pooled / radius
    table = (
        lax.dot_general(vector, vector, NT, precision=HI, preferred_element_type=F32) * INV_T
    )
    row = lax.broadcasted_iota(jnp.int32, (slides, slides), 0)
    col = lax.broadcasted_iota(jnp.int32, (slides, slides), 1)
    positive = jnp.where(row == partner[...], 1.0, 0.0)
    exps = jnp.where(row != col, jnp.exp(table), 0.0)
    normaliser = jnp.sum(exps, axis=-1, keepdims=True)
    losses = jnp.log(normaliser) - jnp.sum(positive * table, axis=-1, keepdims=True)
    coefficients = exps / normaliser - positive
    both = coefficients + coefficients.T
    embed_grad = jnp.dot(both, vector, precision=HI, preferred_element_type=F32) * INV_T
    projection = jnp.sum(pooled * embed_grad, axis=-1, keepdims=True)
    pooled_grad = SCALE * (
        embed_grad / radius - pooled * (projection / (radius * radius * radius))
    )
    dots = jnp.sum(pooled_grad * pooled, axis=-1, keepdims=True)
    index = lax.broadcasted_iota(jnp.int32, (slides, 1), 0)
    fetch.wait()
    for s in range(S):
        mine = index == position * S + s

        def pick(values):
            return jnp.sum(jnp.where(mine, values, 0.0), axis=0, keepdims=True)

        vector_out[s : s + 1, :] = pick(vector)
        loss_out[s] = jnp.sum(jnp.where(mine, losses, 0.0))
        grad = pick(pooled_grad)
        dot = pick(dots)
        total = pick(totals)
        rows = slice(s * HALF, s * HALF + HALF)
        aligned = jnp.sum(embedded[rows, :].astype(F32) * grad, axis=-1, keepdims=True)
        share = weight[rows, :] / total
        score = share * (aligned - dot)
        moved = (slope[rows, :].astype(F32) * grad).astype(BF)
        back = lax.dot_general(moved, emb[...], NT, preferred_element_type=F32)
        share = jnp.concatenate([share] * (C // LANES), axis=1)
        score = jnp.concatenate([score] * (C // LANES), axis=1)
        fresh = share * back + score * gate_term[rows, :]
        grad_out[s] = fresh.astype(BF).reshape(R, W, C)


HBM = pl.BlockSpec(memory_space=pltpu.HBM)
VM = pl.BlockSpec(memory_space=pltpu.VMEM)
SM = pl.BlockSpec(memory_space=pltpu.SMEM)
PAY = A + LANES


def params(mib):
    return pltpu.CompilerParams(vmem_limit_bytes=mib * 1024 * 1024)


def shards(
    features, tissue, partner, dw_kernel, dw_bias, ln_gain, ln_bias, w_up,
    narrowing_projection_kernel, layer_scale, w_embed, embed_bias, attn_v, attn_u, attn_w,
):
    block = (S, R, W, C)
    strip = (S, R, 8, C)
    masked_shapes = (
        jax.ShapeDtypeStruct(block, BF),
        jax.ShapeDtypeStruct(strip, BF),
        jax.ShapeDtypeStruct((N, LANES), F32),
    )
    masked, edge, flags = pl.pallas_call(
        mask_kernel,
        out_shape=masked_shapes,
        in_specs=[HBM, VM],
        out_specs=(HBM, HBM, HBM),
        scratch_shapes=[pltpu.VMEM(block, BF)]
        + [pltpu.VMEM(x.shape, x.dtype) for x in masked_shapes]
        + [pltpu.SemaphoreType.DMA((2 * S * R + 2,))],
        compiler_params=params(60),
        name="mask",
    )(features, tissue.transpose(1, 0, 2))
    tile = ("z", "xl")
    count = lax.axis_size(tile)
    upward = [(i, i + 1) for i in range(count - 1)]
    downward = [(i + 1, i) for i in range(count - 1)]
    above = lax.ppermute(masked, tile, upward)
    below = lax.ppermute(masked, tile, downward)
    edge_own = lax.ppermute(edge, "section", [(0, 1), (1, 0)])
    every = ("section",) + tile
    edge_above = lax.ppermute(
        edge, every, [(c * count + i, (1 - c) * count + i + 1) for c in range(2) for i in range(count - 1)]
    )
    edge_below = lax.ppermute(
        edge, every, [(c * count + i + 1, (1 - c) * count + i) for c in range(2) for i in range(count - 1)]
    )
    depth = lax.axis_size("z")

    operands = (
        masked, above, below, edge_own, edge_above, edge_below, flags,
        dw_kernel, dw_bias, ln_gain, ln_bias, layer_scale, embed_bias, attn_w,
        w_up, narrowing_projection_kernel, w_embed, attn_v, attn_u,
    )
    forward_shapes = (
        jax.ShapeDtypeStruct((depth, S, PAY), F32),
        jax.ShapeDtypeStruct((N, A), BF),
        jax.ShapeDtypeStruct((N, A), BF),
        jax.ShapeDtypeStruct((N, LANES), F32),
        jax.ShapeDtypeStruct((N, AH), BF),
        jax.ShapeDtypeStruct((N, AH), BF),
    )
    payload, embedded, slope, weight, gate_v, gate_u = pl.pallas_call(
        forward_kernel,
        out_shape=forward_shapes,
        in_specs=[HBM] * len(operands),
        out_specs=[HBM] * len(forward_shapes),
        scratch_shapes=[pltpu.VMEM(x.shape, x.dtype) for x in operands + forward_shapes]
        + [
            pltpu.VMEM((S, 3 * R, PW, C), F32),
            pltpu.VMEM((R, 7, PW, LANES), F32),
            pltpu.VMEM((N, C), F32),
            pltpu.VMEM((S, PAY), F32),
            pltpu.SemaphoreType.DMA((len(operands) + len(forward_shapes),)),
        ],
        compiler_params=params(60),
        cost_estimate=pl.CostEstimate(flops=2 * 10**9, bytes_accessed=8 * 10**6, transcendentals=10**6),
        name="forward",
    )(*operands)
    gate_term = pl.pallas_call(
        slope_kernel,
        out_shape=jax.ShapeDtypeStruct((N, C), F32),
        in_specs=[VM] * 3 + [HBM] * 3,
        out_specs=VM,
        scratch_shapes=[
            pltpu.VMEM((C, A), BF),
            pltpu.VMEM((A, AH), BF),
            pltpu.VMEM((A, AH), BF),
            pltpu.SemaphoreType.DMA((3,)),
        ],
        compiler_params=params(24),
        cost_estimate=pl.CostEstimate(flops=10**9, bytes_accessed=4 * 10**6, transcendentals=0),
        name="gate_term",
    )(gate_v, gate_u, slope, w_embed, attn_v, attn_u)

    plane = ("section", "xl", "set")
    received = lax.all_to_all(payload, "z", 0, 0, tiled=True)
    payload = pl.pallas_call(
        sum_kernel,
        out_shape=jax.ShapeDtypeStruct((lax.axis_size(plane), S, PAY), F32),
        in_specs=[VM, HBM],
        out_specs=VM,
        compiler_params=params(24),
        name="add_up",
    )(received, gate_term)
    received = lax.all_to_all(payload, plane, 0, 0, tiled=True)
    slides = partner.shape[0]
    return pl.pallas_call(
        final_kernel,
        out_shape=(
            jax.ShapeDtypeStruct((S,), F32),
            jax.ShapeDtypeStruct((S, A), F32),
            jax.ShapeDtypeStruct((S, R, W, C), BF),
        ),
        in_specs=[VM] * 6 + [HBM],
        out_specs=(SM, VM, VM),
        scratch_shapes=[
            pltpu.VMEM((slides, PAY), F32),
            pltpu.VMEM((C, A), BF),
            pltpu.SemaphoreType.DMA(()),
        ],
        compiler_params=params(24),
        name="final",
    )(received, partner.reshape(1, slides), embedded, slope, weight, gate_term, w_embed)


def solution(mesh):
    section, tile, groups = mesh.devices.shape
    fine = Mesh(
        mesh.devices.reshape(section, tile // 2, 2, groups), ("section", "z", "xl", "set")
    )
    tiles = ("z", "xl")
    placed = (P("set", tiles, "section", None), P("set", tiles, "section")) + (P(),) * 13
    return jax.shard_map(
        shards,
        mesh=fine,
        in_specs=placed,
        out_specs=(P("set"), P("set", None), P("set", tiles, "section", None)),
        check_vma=False,
    )
```

```python
import jax
import jax.numpy as jnp
from jax import lax
from jax.experimental import pallas as pl
from jax.experimental.pallas import tpu as pltpu
from jax.sharding import Mesh
from jax.sharding import PartitionSpec as P

C = 384
HID = 1536
A = 1024
AH = 256
S = 2
R = 3
W = 64
N = S * R * W
PW = W + 8
LANES = 128
HALF = S * R * W // S
INV_T = 10.0
SCALE = 65536.0
RSQRT2 = 0.7071067811865476
RSQRT2PI = 0.3989422804014327
NT = (((1,), (1,)), ((), ()))
HI = lax.Precision.HIGHEST
F32 = jnp.float32
BF = jnp.bfloat16


def copies_between(pairs, sems, first=0):
    return [
        pltpu.make_async_copy(src, dst, sems.at[first + i]) for i, (src, dst) in enumerate(pairs)
    ]


def mask_kernel(
    features_hbm, tissue, masked_hbm, edge_hbm, flags_hbm, features, masked, edge, flags, sems
):
    where = [(s, r) for s in range(S) for r in range(R)]
    arrive = copies_between([(features_hbm.at[p], features.at[p]) for p in where], sems)
    leave = copies_between([(masked.at[p], masked_hbm.at[p]) for p in where], sems, S * R)
    last_out = copies_between([(edge, edge_hbm), (flags, flags_hbm)], sems, 2 * S * R)
    for c in arrive:
        c.start()
    side = lax.axis_index("section")
    place = lax.broadcasted_iota(jnp.int32, (8, C), 0)
    first = jnp.where((place < 3) & (side == 1), 1.0, 0.0)
    last = jnp.where((place >= 5) & (side == 0), 1.0, 0.0)
    rows = [tissue[r, s : s + 1, :].astype(F32) for s, r in where]
    turned = jnp.concatenate(rows + rows[:2], axis=0).T
    for i, (s, r) in enumerate(where):
        here = jnp.broadcast_to(turned[:, i : i + 1], (W, LANES))
        flags[i * W : i * W + W, :] = here
        wide = jnp.concatenate([here] * (C // LANES), axis=1)
        arrive[i].wait()
        values = features[s, r].astype(F32) * wide
        masked[s, r] = values.astype(BF)
        leave[i].start()
        edge[s, r] = (values[:8] * first + values[W - 8 :] * last).astype(BF)
    for c in last_out:
        c.start()
    for c in leave + last_out:
        c.wait()


def fill(grid_ref, at, block, edge):
    for s in range(S):
        for r in range(R):
            grid_ref[s, at + r, 0:W, :] = block[s, r].astype(F32)
            grid_ref[s, at + r, W:PW, :] = edge[s, r].astype(F32)


def convolve(grid_ref, acc_ref, conv_ref, dw_k, first, count, seed):
    odd = lax.axis_index("xl") == 1

    def turn(i, last):
        return jnp.where(odd, last - i, i)

    def conv_lane(step, carry):
        s = step // (C // LANES)
        lane = pl.multiple_of(lax.rem(step, C // LANES) * LANES, LANES)
        for col in range(PW // 8):
            cols = slice(col * 8, col * 8 + 8)
            rows = [
                grid_ref[s, base + turn(m, R - 1), cols, pl.ds(lane, LANES)]
                for base in range(0, count, R)
                for m in range(R)
            ]
            for b in range(7):
                sums = [None] * R
                for a in range(7):
                    pairs = [(a + n - first, n) for n in range(R) if 0 <= a + n - first < count]
                    if not pairs:
                        continue
                    k = dw_k[turn(a, 6), b, pl.ds(lane, LANES)].reshape(1, LANES)
                    for row, n in pairs:
                        term = rows[row] * k
                        sums[n] = term if sums[n] is None else sums[n] + term
                for n in range(R):
                    acc_ref[n, b, cols, :] = sums[n]
        for n in range(R):
            total = acc_ref[n, 3]
            for b in (0, 1, 2, 4, 5, 6):
                total = total + pltpu.roll(acc_ref[n, b], (3 - b) % PW, 0)
            at = pl.multiple_of(s * R * W + turn(n, R - 1) * W, W)
            where = (pl.ds(at, W), pl.ds(lane, LANES))
            total = total[0:W]
            conv_ref[where] = total if seed is None else total + seed[where]
        return carry

    lax.fori_loop(0, S * (C // LANES), conv_lane, 0)


def near_kernel(
    own_hbm, edge_own_hbm, near_hbm, edge_near_hbm, dw_k_hbm, partial_hbm,
    own, edge_own, near, edge_near, dw_k, partial, grid_ref, acc_ref, sems,
):
    arrive = copies_between(
        (
            (own_hbm, own), (edge_own_hbm, edge_own), (near_hbm, near),
            (edge_near_hbm, edge_near), (dw_k_hbm, dw_k),
        ),
        sems,
    )
    for c in arrive:
        c.start()
    for c in arrive:
        c.wait()
    fill(grid_ref, 0, own, edge_own)
    fill(grid_ref, R, near, edge_near)
    convolve(grid_ref, acc_ref, partial, dw_k, R, 2 * R, None)
    leave = pltpu.make_async_copy(partial, partial_hbm, sems.at[5])
    leave.start()
    leave.wait()


def forward_kernel(
    far_hbm, edge_far_hbm, partial_hbm, own_hbm, flags_hbm,
    dw_k_hbm, dw_b_hbm, ln_g_hbm, ln_b_hbm, scale_hbm, e_bias_hbm, a_w_hbm,
    up_hbm, down_hbm, emb_hbm, v_hbm, u_hbm,
    payload_hbm, embedded_hbm, slope_hbm, weight_hbm, gate_v_hbm, gate_u_hbm,
    far, edge_far, partial, own, flags,
    dw_k, dw_b, ln_g, ln_b, scale, e_bias, a_w, up, down, emb, att_v, att_u,
    payload, embedded_out, slope_out, weight_out, gate_v_out, gate_u_out,
    grid_ref, acc_ref, conv_ref, sums_ref, sems,
):
    blocks = copies_between(
        (
            (far_hbm, far), (edge_far_hbm, edge_far), (dw_k_hbm, dw_k), (partial_hbm, partial),
        ),
        sems,
    )
    small = copies_between(
        (
            (own_hbm, own), (dw_b_hbm, dw_b), (ln_g_hbm, ln_g), (ln_b_hbm, ln_b),
            (scale_hbm, scale), (e_bias_hbm, e_bias), (a_w_hbm, a_w), (flags_hbm, flags),
        ),
        sems,
        4,
    )
    copies = copies_between(
        ((up_hbm, up), (down_hbm, down), (emb_hbm, emb), (v_hbm, att_v), (u_hbm, att_u)), sems, 12
    )
    results = copies_between(
        (
            (embedded_out, embedded_hbm), (slope_out, slope_hbm), (payload, payload_hbm),
            (weight_out, weight_hbm), (gate_v_out, gate_v_hbm), (gate_u_out, gate_u_hbm),
        ),
        sems,
        17,
    )
    for c in blocks + small + copies:
        c.start()
    for c in blocks:
        c.wait()
    fill(grid_ref, 0, far, edge_far)
    convolve(grid_ref, acc_ref, conv_ref, dw_k, 0, R, partial)
    for c in small:
        c.wait()
    conv = conv_ref[...] + dw_b[...].reshape(1, -1)
    centre = jnp.mean(conv, axis=-1, keepdims=True)
    moved = conv - centre
    spread = jnp.mean(moved * moved, axis=-1, keepdims=True)
    normed = (moved * lax.rsqrt(spread + 1e-06) * ln_g[...].reshape(1, -1) + ln_b[...].reshape(1, -1)).astype(BF)
    copies[0].wait()
    copies[1].wait()
    branch = jnp.zeros((N, C), F32)
    step = 384
    for h in range(0, HID, step):
        raised = jnp.dot(normed, up[:, h : h + step], preferred_element_type=F32)
        hidden = (0.5 * raised * (1.0 + lax.erf(raised * RSQRT2))).astype(BF)
        branch = branch + jnp.dot(hidden, down[h : h + step, :], preferred_element_type=F32)
    tissue = flags[...]
    wide = jnp.concatenate([tissue] * (C // LANES), axis=1)
    masked = own[...].reshape(N, C).astype(F32)
    trunk = ((masked + scale[...].reshape(1, -1) * branch) * wide).astype(BF)
    copies[2].wait()
    copies[3].wait()
    copies[4].wait()
    logits_v = jnp.zeros((N, AH), F32)
    logits_u = jnp.zeros((N, AH), F32)
    step = 256
    for h in range(0, A, step):
        cols = slice(h, h + step)
        pre = jnp.dot(trunk, emb[:, cols], preferred_element_type=F32) + e_bias[cols].reshape(1, -1)
        cdf = 0.5 * (1.0 + lax.erf(pre * RSQRT2))
        slope = cdf + pre * (RSQRT2PI * jnp.exp(-0.5 * pre * pre))
        out = (pre * cdf).astype(BF)
        embedded_out[:, cols] = out
        slope_out[:, cols] = slope.astype(BF)
        logits_v = logits_v + jnp.dot(out, att_v[cols, :], preferred_element_type=F32)
        logits_u = logits_u + jnp.dot(out, att_u[cols, :], preferred_element_type=F32)
    results[0].start()
    results[1].start()
    tangent = jnp.tanh(logits_v)
    opening = jax.nn.sigmoid(logits_u)
    aw = a_w[...].reshape(1, -1)
    product = tangent * opening * aw
    scores = jnp.sum(product, axis=-1, keepdims=True)
    weight = tissue * jnp.exp(scores)
    weight_out[...] = weight
    results[3].start()
    for s in range(S):
        rows = slice(s * HALF, s * HALF + HALF)
        w_here = weight[rows, :]
        for k in range(A // LANES):
            cols = slice(k * LANES, k * LANES + LANES)
            part = jnp.sum(w_here * embedded_out[rows, cols].astype(F32), axis=0, keepdims=True)
            sums_ref[s : s + 1, cols] = part
        sums_ref[s : s + 1, A:] = jnp.sum(w_here, axis=0, keepdims=True)
    payload[...] = jnp.broadcast_to(sums_ref[...][None], payload.shape)
    results[2].start()
    gate_v_out[...] = (aw * opening * (1.0 - tangent * tangent)).astype(BF)
    gate_u_out[...] = (product * (1.0 - opening)).astype(BF)
    results[4].start()
    results[5].start()
    for c in results:
        c.wait()


def slope_kernel(
    gate_v, gate_u, slope, emb_hbm, v_hbm, u_hbm, out, emb, att_v, att_u, sems
):
    copies = [
        pltpu.make_async_copy(src, dst, sems.at[i])
        for i, (src, dst) in enumerate(((v_hbm, att_v), (u_hbm, att_u), (emb_hbm, emb)))
    ]
    for c in copies:
        c.start()
    for c in copies:
        c.wait()
    total = jnp.zeros((N, C), F32)
    step = 256
    for h in range(0, A, step):
        cols = slice(h, h + step)
        back = lax.dot_general(gate_v[...], att_v[cols, :], NT, preferred_element_type=F32)
        back = back + lax.dot_general(gate_u[...], att_u[cols, :], NT, preferred_element_type=F32)
        back = (back * slope[:, cols].astype(F32)).astype(BF)
        total = total + lax.dot_general(back, emb[:, cols], NT, preferred_element_type=F32)
    out[...] = total


def sum_kernel(received, ahead, payload):
    total = jnp.sum(received[...], axis=0)
    payload[...] = jnp.broadcast_to(total[None], payload.shape)


def final_kernel(
    received, partner, embedded, slope, weight, gate_term, emb_hbm,
    loss_out, vector_out, grad_hbm, grad_out, sums_ref, emb, sems,
):
    fetch = pltpu.make_async_copy(emb_hbm, emb, sems.at[S])
    leave = copies_between([(grad_out.at[s], grad_hbm.at[s]) for s in range(S)], sems)
    fetch.start()
    position = lax.axis_index("set")
    slides = sums_ref.shape[0]
    groups = slides // S
    for g in range(groups):
        gathered = received[g]
        for part in range(1, received.shape[0] // groups):
            gathered = gathered + received[part * groups + g]
        sums_ref[g * S : g * S + S, :] = gathered
    totals = sums_ref[:, A:]
    pooled = sums_ref[:, :A] / totals[:, :1]
    radius = jnp.sqrt(jnp.sum(pooled * pooled, axis=-1, keepdims=True) + 1e-06)
    vector = pooled / radius
    table = (
        lax.dot_general(vector, vector, NT, precision=HI, preferred_element_type=F32) * INV_T
    )
    row = lax.broadcasted_iota(jnp.int32, (slides, slides), 0)
    col = lax.broadcasted_iota(jnp.int32, (slides, slides), 1)
    positive = jnp.where(row == partner[...], 1.0, 0.0)
    exps = jnp.where(row != col, jnp.exp(table), 0.0)
    normaliser = jnp.sum(exps, axis=-1, keepdims=True)
    losses = jnp.log(normaliser) - jnp.sum(positive * table, axis=-1, keepdims=True)
    coefficients = exps / normaliser - positive
    both = coefficients + coefficients.T
    embed_grad = jnp.dot(both, vector, precision=HI, preferred_element_type=F32) * INV_T
    projection = jnp.sum(pooled * embed_grad, axis=-1, keepdims=True)
    pooled_grad = SCALE * (
        embed_grad / radius - pooled * (projection / (radius * radius * radius))
    )
    dots = jnp.sum(pooled_grad * pooled, axis=-1, keepdims=True)
    index = lax.broadcasted_iota(jnp.int32, (slides, 1), 0)
    fetch.wait()
    for s in range(S):
        mine = index == position * S + s

        def pick(values):
            return jnp.sum(jnp.where(mine, values, 0.0), axis=0, keepdims=True)

        vector_out[s : s + 1, :] = pick(vector)
        loss_out[s] = jnp.sum(jnp.where(mine, losses, 0.0))
        grad = pick(pooled_grad)
        dot = pick(dots)
        total = pick(totals)
        rows = slice(s * HALF, s * HALF + HALF)
        aligned = jnp.sum(embedded[rows, :].astype(F32) * grad, axis=-1, keepdims=True)
        share = weight[rows, :] / total
        score = share * (aligned - dot)
        moved = (slope[rows, :].astype(F32) * grad).astype(BF)
        back = lax.dot_general(moved, emb[...], NT, preferred_element_type=F32)
        share = jnp.concatenate([share] * (C // LANES), axis=1)
        score = jnp.concatenate([score] * (C // LANES), axis=1)
        fresh = share * back + score * gate_term[rows, :]
        grad_out[s] = fresh.astype(BF).reshape(R, W, C)
        leave[s].start()
    for c in leave:
        c.wait()


HBM = pl.BlockSpec(memory_space=pltpu.HBM)
VM = pl.BlockSpec(memory_space=pltpu.VMEM)
SM = pl.BlockSpec(memory_space=pltpu.SMEM)
PAY = A + LANES


def params(mib):
    return pltpu.CompilerParams(vmem_limit_bytes=mib * 1024 * 1024)


def shards(
    features, tissue, partner, dw_kernel, dw_bias, ln_gain, ln_bias, w_up,
    narrowing_projection_kernel, layer_scale, w_embed, embed_bias, attn_v, attn_u, attn_w,
):
    block = (S, R, W, C)
    strip = (S, R, 8, C)
    masked_shapes = (
        jax.ShapeDtypeStruct(block, BF),
        jax.ShapeDtypeStruct(strip, BF),
        jax.ShapeDtypeStruct((N, LANES), F32),
    )
    masked, edge, flags = pl.pallas_call(
        mask_kernel,
        out_shape=masked_shapes,
        in_specs=[HBM, VM],
        out_specs=(HBM, HBM, HBM),
        scratch_shapes=[pltpu.VMEM(block, BF)]
        + [pltpu.VMEM(x.shape, x.dtype) for x in masked_shapes]
        + [pltpu.SemaphoreType.DMA((2 * S * R + 2,))],
        compiler_params=params(60),
        name="mask",
    )(features, tissue.transpose(1, 0, 2))
    tile = ("z", "xl")
    count = lax.axis_size(tile)
    nearby = [(i, i ^ 1) for i in range(count)]
    away = [(i, i + 1 if i % 2 else i - 1) for i in range(1, count - 1)]
    every = ("section",) + tile

    def crossed(moves):
        return [(c * count + i, (1 - c) * count + j) for c in range(2) for i, j in moves]

    far = lax.ppermute(masked, tile, away)
    near = lax.ppermute(masked, tile, nearby)
    edge_far = lax.ppermute(edge, every, crossed(away))
    edge_near = lax.ppermute(edge, every, crossed(nearby))
    edge_own = lax.ppermute(edge, "section", [(0, 1), (1, 0)])
    depth = lax.axis_size("z")

    sources = (masked, edge_own, near, edge_near, dw_kernel)
    partial = jax.ShapeDtypeStruct((N, C), F32)
    partial = pl.pallas_call(
        near_kernel,
        out_shape=partial,
        in_specs=[HBM] * len(sources),
        out_specs=HBM,
        scratch_shapes=[pltpu.VMEM(x.shape, x.dtype) for x in sources + (partial,)]
        + [
            pltpu.VMEM((S, 2 * R, PW, C), F32),
            pltpu.VMEM((R, 7, PW, LANES), F32),
            pltpu.SemaphoreType.DMA((6,)),
        ],
        compiler_params=params(64),
        cost_estimate=pl.CostEstimate(flops=10**8, bytes_accessed=2 * 10**6, transcendentals=0),
        name="near",
    )(*sources)
    operands = (
        far, edge_far, partial, masked, flags,
        dw_kernel, dw_bias, ln_gain, ln_bias, layer_scale, embed_bias, attn_w,
        w_up, narrowing_projection_kernel, w_embed, attn_v, attn_u,
    )
    forward_shapes = (
        jax.ShapeDtypeStruct((depth, S, PAY), F32),
        jax.ShapeDtypeStruct((N, A), BF),
        jax.ShapeDtypeStruct((N, A), BF),
        jax.ShapeDtypeStruct((N, LANES), F32),
        jax.ShapeDtypeStruct((N, AH), BF),
        jax.ShapeDtypeStruct((N, AH), BF),
    )
    payload, embedded, slope, weight, gate_v, gate_u = pl.pallas_call(
        forward_kernel,
        out_shape=forward_shapes,
        in_specs=[HBM] * len(operands),
        out_specs=[HBM] * len(forward_shapes),
        scratch_shapes=[pltpu.VMEM(x.shape, x.dtype) for x in operands + forward_shapes]
        + [
            pltpu.VMEM((S, R, PW, C), F32),
            pltpu.VMEM((R, 7, PW, LANES), F32),
            pltpu.VMEM((N, C), F32),
            pltpu.VMEM((S, PAY), F32),
            pltpu.SemaphoreType.DMA((len(operands) + len(forward_shapes),)),
        ],
        compiler_params=params(60),
        cost_estimate=pl.CostEstimate(flops=2 * 10**9, bytes_accessed=8 * 10**6, transcendentals=10**6),
        name="forward",
    )(*operands)
    gate_term = pl.pallas_call(
        slope_kernel,
        out_shape=jax.ShapeDtypeStruct((N, C), F32),
        in_specs=[VM] * 3 + [HBM] * 3,
        out_specs=VM,
        scratch_shapes=[
            pltpu.VMEM((C, A), BF),
            pltpu.VMEM((A, AH), BF),
            pltpu.VMEM((A, AH), BF),
            pltpu.SemaphoreType.DMA((3,)),
        ],
        compiler_params=params(24),
        cost_estimate=pl.CostEstimate(flops=10**9, bytes_accessed=4 * 10**6, transcendentals=0),
        name="gate_term",
    )(gate_v, gate_u, slope, w_embed, attn_v, attn_u)

    plane = ("section", "xl", "set")
    received = lax.all_to_all(payload, "z", 0, 0, tiled=True)
    payload = pl.pallas_call(
        sum_kernel,
        out_shape=jax.ShapeDtypeStruct((lax.axis_size(plane), S, PAY), F32),
        in_specs=[VM, HBM],
        out_specs=VM,
        compiler_params=params(24),
        name="add_up",
    )(received, gate_term)
    received = lax.all_to_all(payload, plane, 0, 0, tiled=True)
    slides = partner.shape[0]
    return pl.pallas_call(
        final_kernel,
        out_shape=(
            jax.ShapeDtypeStruct((S,), F32),
            jax.ShapeDtypeStruct((S, A), F32),
            jax.ShapeDtypeStruct((S, R, W, C), BF),
        ),
        in_specs=[VM] * 6 + [HBM],
        out_specs=(SM, VM, HBM),
        scratch_shapes=[
            pltpu.VMEM(block, BF),
            pltpu.VMEM((slides, PAY), F32),
            pltpu.VMEM((C, A), BF),
            pltpu.SemaphoreType.DMA((S + 1,)),
        ],
        compiler_params=params(24),
        name="final",
    )(received, partner.reshape(1, slides), embedded, slope, weight, gate_term, w_embed)


def solution(mesh):
    section, tile, groups = mesh.devices.shape
    fine = Mesh(
        mesh.devices.reshape(section, tile // 2, 2, groups), ("section", "z", "xl", "set")
    )
    tiles = ("z", "xl")
    placed = (P("set", tiles, "section", None), P("set", tiles, "section")) + (P(),) * 13
    return jax.shard_map(
        shards,
        mesh=fine,
        in_specs=placed,
        out_specs=(P("set"), P("set", None), P("set", tiles, "section", None)),
        check_vma=False,
    )
```

```python
import jax
import jax.numpy as jnp
from jax import lax
from jax.experimental import pallas as pl
from jax.experimental.pallas import tpu as pltpu
from jax.sharding import Mesh
from jax.sharding import PartitionSpec as P

C = 384
HID = 1536
A = 1024
AH = 256
S = 2
R = 3
W = 64
N = S * R * W
PW = W + 8
LANES = 128
HALF = S * R * W // S
INV_T = 10.0
SCALE = 65536.0
RSQRT2 = 0.7071067811865476
RSQRT2PI = 0.3989422804014327
NT = (((1,), (1,)), ((), ()))
HI = lax.Precision.HIGHEST
F32 = jnp.float32
BF = jnp.bfloat16


def copies_between(pairs, sems, first=0):
    return [
        pltpu.make_async_copy(src, dst, sems.at[first + i]) for i, (src, dst) in enumerate(pairs)
    ]


def mask_kernel(
    features_hbm, tissue_hbm, masked_hbm, edge_hbm, flags_hbm,
    features, tissue, masked, edge, flags, sems,
):
    first_in = pltpu.make_async_copy(tissue_hbm, tissue, sems.at[2 * S])
    arrive = copies_between([(features_hbm.at[s], features.at[s]) for s in range(S)], sems)
    leave = copies_between([(masked.at[s], masked_hbm.at[s]) for s in range(S)], sems, S)
    last_out = copies_between([(edge, edge_hbm), (flags, flags_hbm)], sems, 2 * S + 1)
    first_in.start()
    for c in arrive:
        c.start()
    side = lax.axis_index("section")
    place = lax.broadcasted_iota(jnp.int32, (8, C), 0)
    first = jnp.where((place < 3) & (side == 1), 1.0, 0.0)
    last = jnp.where((place >= 5) & (side == 0), 1.0, 0.0)
    first_in.wait()
    rows = [tissue[r, s : s + 1, :].astype(F32) for s in range(S) for r in range(R)]
    turned = jnp.concatenate(rows + rows[:2], axis=0).T
    for s in range(S):
        arrive[s].wait()
        for r in range(R):
            i = s * R + r
            here = jnp.broadcast_to(turned[:, i : i + 1], (W, LANES))
            flags[i * W : i * W + W, :] = here
            wide = jnp.concatenate([here] * (C // LANES), axis=1)
            values = features[s, r].astype(F32) * wide
            masked[s, r] = values.astype(BF)
            edge[s, r] = (values[:8] * first + values[W - 8 :] * last).astype(BF)
        leave[s].start()
    for c in last_out:
        c.start()
    for c in leave + last_out:
        c.wait()


def fill(grid_ref, at, block, edge):
    for s in range(S):
        for r in range(R):
            grid_ref[s, at + r, 0:W, :] = block[s, r].astype(F32)
            grid_ref[s, at + r, W:PW, :] = edge[s, r].astype(F32)


def convolve(grid_ref, acc_ref, conv_ref, dw_k, places, seed):
    def conv_lane(step, carry):
        s = step // (C // LANES)
        lane = pl.multiple_of(lax.rem(step, C // LANES) * LANES, LANES)
        for col in range(PW // 8):
            cols = slice(col * 8, col * 8 + 8)
            rows = [grid_ref[s, r, cols, pl.ds(lane, LANES)] for r in range(len(places))]
            for b in range(7):
                sums = [None] * R
                for a in range(7):
                    pairs = [(places.index(a + i), i) for i in range(R) if a + i in places]
                    if not pairs:
                        continue
                    k = dw_k[a, b, pl.ds(lane, LANES)].reshape(1, LANES)
                    for row, i in pairs:
                        term = rows[row] * k
                        sums[i] = term if sums[i] is None else sums[i] + term
                for i in range(R):
                    acc_ref[i, b, cols, :] = sums[i]
        for i in range(R):
            total = acc_ref[i, 3]
            for b in (0, 1, 2, 4, 5, 6):
                total = total + pltpu.roll(acc_ref[i, b], (3 - b) % PW, 0)
            at = pl.multiple_of(s * R * W + i * W, W)
            where = (pl.ds(at, W), pl.ds(lane, LANES))
            total = total[0:W]
            conv_ref[where] = total if seed is None else total + seed[where]
        return carry

    lax.fori_loop(0, S * (C // LANES), conv_lane, 0)


def own_kernel(
    own_hbm, edge_hbm, dw_k_hbm, partial_hbm, own, edge, dw_k, partial, grid_ref, acc_ref, sems
):
    arrive = copies_between(((own_hbm, own), (edge_hbm, edge), (dw_k_hbm, dw_k)), sems)
    for c in arrive:
        c.start()
    for c in arrive:
        c.wait()
    fill(grid_ref, 0, own, edge)
    convolve(grid_ref, acc_ref, partial, dw_k, (3, 4, 5), None)
    leave = pltpu.make_async_copy(partial, partial_hbm, sems.at[3])
    leave.start()
    leave.wait()


def forward_kernel(
    above_hbm, edge_above_hbm, below_hbm, edge_below_hbm, dw_k_hbm, partial_hbm, own_hbm,
    flags_hbm, dw_b_hbm, ln_g_hbm, ln_b_hbm, scale_hbm, e_bias_hbm, a_w_hbm,
    up_hbm, down_hbm, emb_hbm, v_hbm, u_hbm,
    payload_hbm, embedded_hbm, slope_hbm, weight_hbm, gate_v_hbm, gate_u_hbm,
    above, edge_above, below, edge_below, dw_k, partial, own,
    flags, dw_b, ln_g, ln_b, scale, e_bias, a_w, up, down, emb, att_v, att_u,
    payload, embedded_out, slope_out, weight_out, gate_v_out, gate_u_out,
    grid_ref, acc_ref, conv_ref, sums_ref, sems,
):
    blocks = copies_between(
        (
            (above_hbm, above), (edge_above_hbm, edge_above), (below_hbm, below),
            (edge_below_hbm, edge_below), (dw_k_hbm, dw_k), (partial_hbm, partial),
        ),
        sems,
    )
    small = copies_between(
        (
            (own_hbm, own), (dw_b_hbm, dw_b), (ln_g_hbm, ln_g), (ln_b_hbm, ln_b),
            (scale_hbm, scale), (e_bias_hbm, e_bias), (a_w_hbm, a_w), (flags_hbm, flags),
        ),
        sems,
        6,
    )
    copies = copies_between(
        ((up_hbm, up), (down_hbm, down), (emb_hbm, emb), (v_hbm, att_v), (u_hbm, att_u)), sems, 14
    )
    embed_step = 512
    halves = [slice(h, h + embed_step) for h in range(0, A, embed_step)]
    early = copies_between(
        [
            (vm.at[:, cols], hbm.at[:, cols])
            for cols in halves
            for vm, hbm in ((embedded_out, embedded_hbm), (slope_out, slope_hbm))
        ],
        sems,
        19,
    )
    results = copies_between(
        (
            (weight_out, weight_hbm), (payload, payload_hbm), (gate_v_out, gate_v_hbm),
            (gate_u_out, gate_u_hbm),
        ),
        sems,
        23,
    )
    for c in blocks:
        c.start()
    for c in blocks:
        c.wait()
    for c in small + copies:
        c.start()
    fill(grid_ref, 0, above, edge_above)
    fill(grid_ref, R, below, edge_below)
    convolve(grid_ref, acc_ref, conv_ref, dw_k, (0, 1, 2, 6, 7, 8), partial)
    for c in small:
        c.wait()
    conv = conv_ref[...] + dw_b[...].reshape(1, -1)
    centre = jnp.mean(conv, axis=-1, keepdims=True)
    moved = conv - centre
    spread = jnp.mean(moved * moved, axis=-1, keepdims=True)
    normed = (moved * lax.rsqrt(spread + 1e-06) * ln_g[...].reshape(1, -1) + ln_b[...].reshape(1, -1)).astype(BF)
    copies[0].wait()
    copies[1].wait()
    branch = jnp.zeros((N, C), F32)
    step = 768
    for h in range(0, HID, step):
        raised = jnp.dot(normed, up[:, h : h + step], preferred_element_type=F32)
        hidden = (0.5 * raised * (1.0 + lax.erf(raised * RSQRT2))).astype(BF)
        branch = branch + jnp.dot(hidden, down[h : h + step, :], preferred_element_type=F32)
    tissue = flags[...]
    wide = jnp.concatenate([tissue] * (C // LANES), axis=1)
    masked = own[...].reshape(N, C).astype(F32)
    trunk = ((masked + scale[...].reshape(1, -1) * branch) * wide).astype(BF)
    copies[2].wait()
    copies[3].wait()
    copies[4].wait()
    logits_v = jnp.zeros((N, AH), F32)
    logits_u = jnp.zeros((N, AH), F32)
    for h, cols in enumerate(halves):
        pre = jnp.dot(trunk, emb[:, cols], preferred_element_type=F32) + e_bias[cols].reshape(1, -1)
        cdf = 0.5 * (1.0 + lax.erf(pre * RSQRT2))
        slope = cdf + pre * (RSQRT2PI * jnp.exp(-0.5 * pre * pre))
        out = (pre * cdf).astype(BF)
        embedded_out[:, cols] = out
        slope_out[:, cols] = slope.astype(BF)
        early[2 * h].start()
        early[2 * h + 1].start()
        logits_v = logits_v + jnp.dot(out, att_v[cols, :], preferred_element_type=F32)
        logits_u = logits_u + jnp.dot(out, att_u[cols, :], preferred_element_type=F32)
    tangent = jnp.tanh(logits_v)
    opening = jax.nn.sigmoid(logits_u)
    aw = a_w[...].reshape(1, -1)
    product = tangent * opening * aw
    scores = jnp.sum(product, axis=-1, keepdims=True)
    weight = tissue * jnp.exp(scores)
    weight_out[...] = weight
    results[0].start()
    for s in range(S):
        rows = slice(s * HALF, s * HALF + HALF)
        w_here = weight[rows, :]
        for k in range(A // LANES):
            cols = slice(k * LANES, k * LANES + LANES)
            part = jnp.sum(w_here * embedded_out[rows, cols].astype(F32), axis=0, keepdims=True)
            sums_ref[s : s + 1, cols] = part
        sums_ref[s : s + 1, A:] = jnp.sum(w_here, axis=0, keepdims=True)
    payload[...] = jnp.broadcast_to(sums_ref[...][None], payload.shape)
    results[1].start()
    gate_v_out[...] = (aw * opening * (1.0 - tangent * tangent)).astype(BF)
    gate_u_out[...] = (product * (1.0 - opening)).astype(BF)
    results[2].start()
    results[3].start()
    for c in early + results:
        c.wait()


def slope_kernel(
    gate_v, gate_u, slope, emb_hbm, v_hbm, u_hbm, out, emb, att_v, att_u, sems
):
    copies = [
        pltpu.make_async_copy(src, dst, sems.at[i])
        for i, (src, dst) in enumerate(((v_hbm, att_v), (u_hbm, att_u), (emb_hbm, emb)))
    ]
    for c in copies:
        c.start()
    for c in copies:
        c.wait()
    total = jnp.zeros((N, C), F32)
    step = 256
    for h in range(0, A, step):
        cols = slice(h, h + step)
        back = lax.dot_general(gate_v[...], att_v[cols, :], NT, preferred_element_type=F32)
        back = back + lax.dot_general(gate_u[...], att_u[cols, :], NT, preferred_element_type=F32)
        back = (back * slope[:, cols].astype(F32)).astype(BF)
        total = total + lax.dot_general(back, emb[:, cols], NT, preferred_element_type=F32)
    out[...] = total


def sum_kernel(received, ahead, payload):
    total = jnp.sum(received[...], axis=0)
    payload[...] = jnp.broadcast_to(total[None], payload.shape)


def final_kernel(
    received, partner, embedded, slope, weight, gate_term, emb_hbm,
    loss_out, vector_out, grad_out, sums_ref, emb, sem,
):
    fetch = pltpu.make_async_copy(emb_hbm, emb, sem)
    fetch.start()
    position = lax.axis_index("set")
    slides = sums_ref.shape[0]
    groups = slides // S
    for g in range(groups):
        gathered = received[g]
        for part in range(1, received.shape[0] // groups):
            gathered = gathered + received[part * groups + g]
        sums_ref[g * S : g * S + S, :] = gathered
    totals = sums_ref[:, A:]
    pooled = sums_ref[:, :A] / totals[:, :1]
    radius = jnp.sqrt(jnp.sum(pooled * pooled, axis=-1, keepdims=True) + 1e-06)
    vector = pooled / radius
    table = (
        lax.dot_general(vector, vector, NT, precision=HI, preferred_element_type=F32) * INV_T
    )
    row = lax.broadcasted_iota(jnp.int32, (slides, slides), 0)
    col = lax.broadcasted_iota(jnp.int32, (slides, slides), 1)
    positive = jnp.where(row == partner[...], 1.0, 0.0)
    exps = jnp.where(row != col, jnp.exp(table), 0.0)
    normaliser = jnp.sum(exps, axis=-1, keepdims=True)
    losses = jnp.log(normaliser) - jnp.sum(positive * table, axis=-1, keepdims=True)
    coefficients = exps / normaliser - positive
    both = coefficients + coefficients.T
    embed_grad = jnp.dot(both, vector, precision=HI, preferred_element_type=F32) * INV_T
    projection = jnp.sum(pooled * embed_grad, axis=-1, keepdims=True)
    pooled_grad = SCALE * (
        embed_grad / radius - pooled * (projection / (radius * radius * radius))
    )
    dots = jnp.sum(pooled_grad * pooled, axis=-1, keepdims=True)
    index = lax.broadcasted_iota(jnp.int32, (slides, 1), 0)
    fetch.wait()
    for s in range(S):
        mine = index == position * S + s

        def pick(values):
            return jnp.sum(jnp.where(mine, values, 0.0), axis=0, keepdims=True)

        vector_out[s : s + 1, :] = pick(vector)
        loss_out[s] = jnp.sum(jnp.where(mine, losses, 0.0))
        grad = pick(pooled_grad)
        dot = pick(dots)
        total = pick(totals)
        rows = slice(s * HALF, s * HALF + HALF)
        aligned = jnp.sum(embedded[rows, :].astype(F32) * grad, axis=-1, keepdims=True)
        share = weight[rows, :] / total
        score = share * (aligned - dot)
        moved = (slope[rows, :].astype(F32) * grad).astype(BF)
        back = lax.dot_general(moved, emb[...], NT, preferred_element_type=F32)
        share = jnp.concatenate([share] * (C // LANES), axis=1)
        score = jnp.concatenate([score] * (C // LANES), axis=1)
        fresh = share * back + score * gate_term[rows, :]
        grad_out[s] = fresh.astype(BF).reshape(R, W, C)


HBM = pl.BlockSpec(memory_space=pltpu.HBM)
VM = pl.BlockSpec(memory_space=pltpu.VMEM)
SM = pl.BlockSpec(memory_space=pltpu.SMEM)
PAY = A + LANES


def params(mib):
    return pltpu.CompilerParams(vmem_limit_bytes=mib * 1024 * 1024)


def shards(
    features, tissue, partner, dw_kernel, dw_bias, ln_gain, ln_bias, w_up,
    narrowing_projection_kernel, layer_scale, w_embed, embed_bias, attn_v, attn_u, attn_w,
):
    block = (S, R, W, C)
    strip = (S, R, 8, C)
    masked_shapes = (
        jax.ShapeDtypeStruct(block, BF),
        jax.ShapeDtypeStruct(strip, BF),
        jax.ShapeDtypeStruct((N, LANES), F32),
    )
    masked, edge, flags = pl.pallas_call(
        mask_kernel,
        out_shape=masked_shapes,
        in_specs=[HBM, HBM],
        out_specs=(HBM, HBM, HBM),
        scratch_shapes=[pltpu.VMEM(block, BF), pltpu.VMEM((R, S, W), jnp.int32)]
        + [pltpu.VMEM(x.shape, x.dtype) for x in masked_shapes]
        + [pltpu.SemaphoreType.DMA((2 * S + 3,))],
        compiler_params=params(60),
        name="mask",
    )(features, tissue.transpose(1, 0, 2))
    tile = ("z", "xl")
    count = lax.axis_size(tile)
    upward = [(i, i + 1) for i in range(count - 1)]
    downward = [(i + 1, i) for i in range(count - 1)]
    above = lax.ppermute(masked, tile, upward)
    below = lax.ppermute(masked, tile, downward)
    edge_own = lax.ppermute(edge, "section", [(0, 1), (1, 0)])
    every = ("section",) + tile
    edge_above = lax.ppermute(
        edge, every, [(c * count + i, (1 - c) * count + i + 1) for c in range(2) for i in range(count - 1)]
    )
    edge_below = lax.ppermute(
        edge, every, [(c * count + i + 1, (1 - c) * count + i) for c in range(2) for i in range(count - 1)]
    )
    depth = lax.axis_size("z")

    sources = (masked, edge_own, dw_kernel)
    partial = jax.ShapeDtypeStruct((N, C), F32)
    partial = pl.pallas_call(
        own_kernel,
        out_shape=partial,
        in_specs=[HBM] * len(sources),
        out_specs=HBM,
        scratch_shapes=[pltpu.VMEM(x.shape, x.dtype) for x in sources + (partial,)]
        + [
            pltpu.VMEM((S, R, PW, C), F32),
            pltpu.VMEM((R, 7, PW, LANES), F32),
            pltpu.SemaphoreType.DMA((4,)),
        ],
        compiler_params=params(64),
        cost_estimate=pl.CostEstimate(flops=10**8, bytes_accessed=2 * 10**6, transcendentals=0),
        name="own_rows",
    )(*sources)
    operands = (
        above, edge_above, below, edge_below, dw_kernel, partial, masked, flags, dw_bias, ln_gain,
        ln_bias, layer_scale, embed_bias, attn_w, w_up, narrowing_projection_kernel, w_embed, attn_v, attn_u,
    )
    forward_shapes = (
        jax.ShapeDtypeStruct((depth, S, PAY), F32),
        jax.ShapeDtypeStruct((N, A), BF),
        jax.ShapeDtypeStruct((N, A), BF),
        jax.ShapeDtypeStruct((N, LANES), F32),
        jax.ShapeDtypeStruct((N, AH), BF),
        jax.ShapeDtypeStruct((N, AH), BF),
    )
    payload, embedded, slope, weight, gate_v, gate_u = pl.pallas_call(
        forward_kernel,
        out_shape=forward_shapes,
        in_specs=[HBM] * len(operands),
        out_specs=[HBM] * len(forward_shapes),
        scratch_shapes=[pltpu.VMEM(x.shape, x.dtype) for x in operands + forward_shapes]
        + [
            pltpu.VMEM((S, 2 * R, PW, C), F32),
            pltpu.VMEM((R, 7, PW, LANES), F32),
            pltpu.VMEM((N, C), F32),
            pltpu.VMEM((S, PAY), F32),
            pltpu.SemaphoreType.DMA((27,)),
        ],
        compiler_params=params(60),
        cost_estimate=pl.CostEstimate(flops=2 * 10**9, bytes_accessed=8 * 10**6, transcendentals=10**6),
        name="forward",
    )(*operands)
    gate_term = pl.pallas_call(
        slope_kernel,
        out_shape=jax.ShapeDtypeStruct((N, C), F32),
        in_specs=[VM] * 3 + [HBM] * 3,
        out_specs=VM,
        scratch_shapes=[
            pltpu.VMEM((C, A), BF),
            pltpu.VMEM((A, AH), BF),
            pltpu.VMEM((A, AH), BF),
            pltpu.SemaphoreType.DMA((3,)),
        ],
        compiler_params=params(24),
        cost_estimate=pl.CostEstimate(flops=10**9, bytes_accessed=4 * 10**6, transcendentals=0),
        name="gate_term",
    )(gate_v, gate_u, slope, w_embed, attn_v, attn_u)

    plane = ("section", "xl", "set")
    received = lax.all_to_all(payload, "z", 0, 0, tiled=True)
    payload = pl.pallas_call(
        sum_kernel,
        out_shape=jax.ShapeDtypeStruct((lax.axis_size(plane), S, PAY), F32),
        in_specs=[VM, HBM],
        out_specs=VM,
        compiler_params=params(24),
        name="add_up",
    )(received, gate_term)
    received = lax.all_to_all(payload, plane, 0, 0, tiled=True)
    slides = partner.shape[0]
    return pl.pallas_call(
        final_kernel,
        out_shape=(
            jax.ShapeDtypeStruct((S,), F32),
            jax.ShapeDtypeStruct((S, A), F32),
            jax.ShapeDtypeStruct((S, R, W, C), BF),
        ),
        in_specs=[VM] * 6 + [HBM],
        out_specs=(SM, VM, VM),
        scratch_shapes=[
            pltpu.VMEM((slides, PAY), F32),
            pltpu.VMEM((C, A), BF),
            pltpu.SemaphoreType.DMA(()),
        ],
        compiler_params=params(24),
        name="final",
    )(received, partner.reshape(1, slides), embedded, slope, weight, gate_term, w_embed)


def solution(mesh):
    section, tile, groups = mesh.devices.shape
    fine = Mesh(
        mesh.devices.reshape(section, tile // 2, 2, groups), ("section", "z", "xl", "set")
    )
    tiles = ("z", "xl")
    placed = (P("set", tiles, "section", None), P("set", tiles, "section")) + (P(),) * 13
    return jax.shard_map(
        shards,
        mesh=fine,
        in_specs=placed,
        out_specs=(P("set"), P("set", None), P("set", tiles, "section", None)),
        check_vma=False,
    )
```

```python
import jax
import jax.numpy as jnp
from jax import lax
from jax.experimental import pallas as pl
from jax.experimental.pallas import tpu as pltpu
from jax.sharding import Mesh
from jax.sharding import PartitionSpec as P

C = 384
HID = 1536
A = 1024
AH = 256
S = 2
R = 3
W = 64
N = S * R * W
PW = W + 8
LANES = 128
HALF = S * R * W // S
INV_T = 10.0
SCALE = 65536.0
RSQRT2 = 0.7071067811865476
RSQRT2PI = 0.3989422804014327
NT = (((1,), (1,)), ((), ()))
HI = lax.Precision.HIGHEST
F32 = jnp.float32
BF = jnp.bfloat16


def copies_between(pairs, sems, first=0):
    return [
        pltpu.make_async_copy(src, dst, sems.at[first + i]) for i, (src, dst) in enumerate(pairs)
    ]


def mask_kernel(
    features_hbm, tissue_hbm, masked_hbm, edge_hbm, flags_hbm,
    features, tissue, masked, edge, flags, sems,
):
    first_in = pltpu.make_async_copy(tissue_hbm, tissue, sems.at[2 * S])
    arrive = copies_between([(features_hbm.at[s], features.at[s]) for s in range(S)], sems)
    leave = copies_between([(masked.at[s], masked_hbm.at[s]) for s in range(S)], sems, S)
    last_out = copies_between([(edge, edge_hbm), (flags, flags_hbm)], sems, 2 * S + 1)
    first_in.start()
    for c in arrive:
        c.start()
    side = lax.axis_index("section")
    place = lax.broadcasted_iota(jnp.int32, (8, C), 0)
    first = jnp.where((place < 3) & (side == 1), 1.0, 0.0)
    last = jnp.where((place >= 5) & (side == 0), 1.0, 0.0)
    first_in.wait()
    rows = [tissue[r, s : s + 1, :].astype(F32) for s in range(S) for r in range(R)]
    turned = jnp.concatenate(rows + rows[:2], axis=0).T
    for s in range(S):
        arrive[s].wait()
        for r in range(R):
            i = s * R + r
            here = jnp.broadcast_to(turned[:, i : i + 1], (W, LANES))
            flags[i * W : i * W + W, :] = here
            wide = jnp.concatenate([here] * (C // LANES), axis=1)
            values = features[s, r].astype(F32) * wide
            masked[s, r] = values.astype(BF)
            edge[s, r] = (values[:8] * first + values[W - 8 :] * last).astype(BF)
        leave[s].start()
    for c in last_out:
        c.start()
    for c in leave + last_out:
        c.wait()


def fill(grid_ref, at, block, edge):
    for s in range(S):
        for r in range(R):
            if block is not None:
                grid_ref[s, at + r, 0:W, :] = block[s, r].astype(F32)
            if edge is not None:
                grid_ref[s, at + r, W:PW, :] = edge[s, r].astype(F32)


def convolve(grid_ref, acc_ref, conv_ref, dw_k, inner, outer, seed):
    def conv_lane(step, carry):
        s = step // (C // LANES)
        lane = pl.multiple_of(lax.rem(step, C // LANES) * LANES, LANES)
        for col in range(PW // 8):
            cols = slice(col * 8, col * 8 + 8)
            places = inner if col < W // 8 else outer
            rows = [grid_ref[s, r, cols, pl.ds(lane, LANES)] for r in places]
            for b in range(7):
                sums = [None] * R
                for a in range(7):
                    pairs = [(places.index(a + i), i) for i in range(R) if a + i in places]
                    if not pairs:
                        continue
                    k = dw_k[a, b, pl.ds(lane, LANES)].reshape(1, LANES)
                    for row, i in pairs:
                        term = rows[row] * k
                        sums[i] = term if sums[i] is None else sums[i] + term
                for i in range(R):
                    empty = sums[i] is None
                    acc_ref[i, b, cols, :] = jnp.zeros((8, LANES), F32) if empty else sums[i]
        for i in range(R):
            total = acc_ref[i, 3]
            for b in (0, 1, 2, 4, 5, 6):
                total = total + pltpu.roll(acc_ref[i, b], (3 - b) % PW, 0)
            at = pl.multiple_of(s * R * W + i * W, W)
            where = (pl.ds(at, W), pl.ds(lane, LANES))
            total = total[0:W]
            conv_ref[where] = total if seed is None else total + seed[where]
        return carry

    lax.fori_loop(0, S * (C // LANES), conv_lane, 0)


def own_kernel(
    own_hbm, dw_k_hbm, partial_hbm, own, dw_k, partial, grid_ref, acc_ref, sems
):
    arrive = copies_between(((own_hbm, own), (dw_k_hbm, dw_k)), sems)
    for c in arrive:
        c.start()
    for c in arrive:
        c.wait()
    fill(grid_ref, R, own, None)
    convolve(grid_ref, acc_ref, partial, dw_k, (3, 4, 5), (), None)
    leave = pltpu.make_async_copy(partial, partial_hbm, sems.at[2])
    leave.start()
    leave.wait()


def forward_kernel(
    edge_own_hbm, above_hbm, edge_above_hbm, below_hbm, edge_below_hbm, dw_k_hbm, partial_hbm, own_hbm,
    flags_hbm, dw_b_hbm, ln_g_hbm, ln_b_hbm, scale_hbm, e_bias_hbm, a_w_hbm,
    up_hbm, down_hbm, emb_hbm, v_hbm, u_hbm,
    payload_hbm, embedded_hbm, slope_hbm, weight_hbm, gate_v_hbm, gate_u_hbm,
    edge_own, above, edge_above, below, edge_below, dw_k, partial, own,
    flags, dw_b, ln_g, ln_b, scale, e_bias, a_w, up, down, emb, att_v, att_u,
    payload, embedded_out, slope_out, weight_out, gate_v_out, gate_u_out,
    grid_ref, acc_ref, conv_ref, sums_ref, sems,
):
    blocks = copies_between(
        (
            (above_hbm, above), (edge_above_hbm, edge_above), (below_hbm, below),
            (edge_below_hbm, edge_below), (edge_own_hbm, edge_own), (dw_k_hbm, dw_k),
            (partial_hbm, partial),
        ),
        sems,
    )
    small = copies_between(
        (
            (own_hbm, own), (dw_b_hbm, dw_b), (ln_g_hbm, ln_g), (ln_b_hbm, ln_b),
            (scale_hbm, scale), (e_bias_hbm, e_bias), (a_w_hbm, a_w), (flags_hbm, flags),
        ),
        sems,
        7,
    )
    copies = copies_between(
        ((up_hbm, up), (down_hbm, down), (emb_hbm, emb), (v_hbm, att_v), (u_hbm, att_u)), sems, 15
    )
    embed_step = 512
    halves = [slice(h, h + embed_step) for h in range(0, A, embed_step)]
    early = copies_between(
        [
            (vm.at[:, cols], hbm.at[:, cols])
            for cols in halves
            for vm, hbm in ((embedded_out, embedded_hbm), (slope_out, slope_hbm))
        ],
        sems,
        20,
    )
    results = copies_between(
        (
            (weight_out, weight_hbm), (payload, payload_hbm), (gate_v_out, gate_v_hbm),
            (gate_u_out, gate_u_hbm),
        ),
        sems,
        24,
    )
    for c in blocks:
        c.start()
    for c in blocks:
        c.wait()
    for c in small + copies:
        c.start()
    fill(grid_ref, 0, above, edge_above)
    fill(grid_ref, R, None, edge_own)
    fill(grid_ref, 2 * R, below, edge_below)
    convolve(
        grid_ref, acc_ref, conv_ref, dw_k, (0, 1, 2, 6, 7, 8), tuple(range(3 * R)), partial
    )
    for c in small:
        c.wait()
    conv = conv_ref[...] + dw_b[...].reshape(1, -1)
    centre = jnp.mean(conv, axis=-1, keepdims=True)
    moved = conv - centre
    spread = jnp.mean(moved * moved, axis=-1, keepdims=True)
    normed = (moved * lax.rsqrt(spread + 1e-06) * ln_g[...].reshape(1, -1) + ln_b[...].reshape(1, -1)).astype(BF)
    copies[0].wait()
    copies[1].wait()
    branch = jnp.zeros((N, C), F32)
    step = 768
    for h in range(0, HID, step):
        raised = jnp.dot(normed, up[:, h : h + step], preferred_element_type=F32)
        hidden = (0.5 * raised * (1.0 + lax.erf(raised * RSQRT2))).astype(BF)
        branch = branch + jnp.dot(hidden, down[h : h + step, :], preferred_element_type=F32)
    tissue = flags[...]
    wide = jnp.concatenate([tissue] * (C // LANES), axis=1)
    masked = own[...].reshape(N, C).astype(F32)
    trunk = ((masked + scale[...].reshape(1, -1) * branch) * wide).astype(BF)
    copies[2].wait()
    copies[3].wait()
    copies[4].wait()
    logits_v = jnp.zeros((N, AH), F32)
    logits_u = jnp.zeros((N, AH), F32)
    for h, cols in enumerate(halves):
        pre = jnp.dot(trunk, emb[:, cols], preferred_element_type=F32) + e_bias[cols].reshape(1, -1)
        cdf = 0.5 * (1.0 + lax.erf(pre * RSQRT2))
        slope = cdf + pre * (RSQRT2PI * jnp.exp(-0.5 * pre * pre))
        out = (pre * cdf).astype(BF)
        embedded_out[:, cols] = out
        slope_out[:, cols] = slope.astype(BF)
        early[2 * h].start()
        early[2 * h + 1].start()
        logits_v = logits_v + jnp.dot(out, att_v[cols, :], preferred_element_type=F32)
        logits_u = logits_u + jnp.dot(out, att_u[cols, :], preferred_element_type=F32)
    tangent = jnp.tanh(logits_v)
    opening = jax.nn.sigmoid(logits_u)
    aw = a_w[...].reshape(1, -1)
    product = tangent * opening * aw
    scores = jnp.sum(product, axis=-1, keepdims=True)
    weight = tissue * jnp.exp(scores)
    weight_out[...] = weight
    results[0].start()
    for s in range(S):
        rows = slice(s * HALF, s * HALF + HALF)
        w_here = weight[rows, :]
        for k in range(A // LANES):
            cols = slice(k * LANES, k * LANES + LANES)
            part = jnp.sum(w_here * embedded_out[rows, cols].astype(F32), axis=0, keepdims=True)
            sums_ref[s : s + 1, cols] = part
        sums_ref[s : s + 1, A:] = jnp.sum(w_here, axis=0, keepdims=True)
    payload[...] = jnp.broadcast_to(sums_ref[...][None], payload.shape)
    results[1].start()
    gate_v_out[...] = (aw * opening * (1.0 - tangent * tangent)).astype(BF)
    gate_u_out[...] = (product * (1.0 - opening)).astype(BF)
    results[2].start()
    results[3].start()
    for c in early + results:
        c.wait()


def slope_kernel(
    gate_v, gate_u, slope, emb_hbm, v_hbm, u_hbm, out, emb, att_v, att_u, sems
):
    copies = [
        pltpu.make_async_copy(src, dst, sems.at[i])
        for i, (src, dst) in enumerate(((v_hbm, att_v), (u_hbm, att_u), (emb_hbm, emb)))
    ]
    for c in copies:
        c.start()
    for c in copies:
        c.wait()
    total = jnp.zeros((N, C), F32)
    step = 256
    for h in range(0, A, step):
        cols = slice(h, h + step)
        back = lax.dot_general(gate_v[...], att_v[cols, :], NT, preferred_element_type=F32)
        back = back + lax.dot_general(gate_u[...], att_u[cols, :], NT, preferred_element_type=F32)
        back = (back * slope[:, cols].astype(F32)).astype(BF)
        total = total + lax.dot_general(back, emb[:, cols], NT, preferred_element_type=F32)
    out[...] = total


def sum_kernel(received, ahead, payload):
    total = jnp.sum(received[...], axis=0)
    payload[...] = jnp.broadcast_to(total[None], payload.shape)


def final_kernel(
    received, partner, embedded, slope, weight, gate_term, emb_hbm,
    loss_out, vector_out, grad_out, sums_ref, emb, sem,
):
    fetch = pltpu.make_async_copy(emb_hbm, emb, sem)
    fetch.start()
    position = lax.axis_index("set")
    slides = sums_ref.shape[0]
    groups = slides // S
    for g in range(groups):
        gathered = received[g]
        for part in range(1, received.shape[0] // groups):
            gathered = gathered + received[part * groups + g]
        sums_ref[g * S : g * S + S, :] = gathered
    totals = sums_ref[:, A:]
    pooled = sums_ref[:, :A] / totals[:, :1]
    radius = jnp.sqrt(jnp.sum(pooled * pooled, axis=-1, keepdims=True) + 1e-06)
    vector = pooled / radius
    table = (
        lax.dot_general(vector, vector, NT, precision=HI, preferred_element_type=F32) * INV_T
    )
    row = lax.broadcasted_iota(jnp.int32, (slides, slides), 0)
    col = lax.broadcasted_iota(jnp.int32, (slides, slides), 1)
    positive = jnp.where(row == partner[...], 1.0, 0.0)
    exps = jnp.where(row != col, jnp.exp(table), 0.0)
    normaliser = jnp.sum(exps, axis=-1, keepdims=True)
    losses = jnp.log(normaliser) - jnp.sum(positive * table, axis=-1, keepdims=True)
    coefficients = exps / normaliser - positive
    both = coefficients + coefficients.T
    embed_grad = jnp.dot(both, vector, precision=HI, preferred_element_type=F32) * INV_T
    projection = jnp.sum(pooled * embed_grad, axis=-1, keepdims=True)
    pooled_grad = SCALE * (
        embed_grad / radius - pooled * (projection / (radius * radius * radius))
    )
    dots = jnp.sum(pooled_grad * pooled, axis=-1, keepdims=True)
    index = lax.broadcasted_iota(jnp.int32, (slides, 1), 0)
    fetch.wait()
    for s in range(S):
        mine = index == position * S + s

        def pick(values):
            return jnp.sum(jnp.where(mine, values, 0.0), axis=0, keepdims=True)

        vector_out[s : s + 1, :] = pick(vector)
        loss_out[s] = jnp.sum(jnp.where(mine, losses, 0.0))
        grad = pick(pooled_grad)
        dot = pick(dots)
        total = pick(totals)
        rows = slice(s * HALF, s * HALF + HALF)
        aligned = jnp.sum(embedded[rows, :].astype(F32) * grad, axis=-1, keepdims=True)
        share = weight[rows, :] / total
        score = share * (aligned - dot)
        moved = (slope[rows, :].astype(F32) * grad).astype(BF)
        back = lax.dot_general(moved, emb[...], NT, preferred_element_type=F32)
        share = jnp.concatenate([share] * (C // LANES), axis=1)
        score = jnp.concatenate([score] * (C // LANES), axis=1)
        fresh = share * back + score * gate_term[rows, :]
        grad_out[s] = fresh.astype(BF).reshape(R, W, C)


HBM = pl.BlockSpec(memory_space=pltpu.HBM)
VM = pl.BlockSpec(memory_space=pltpu.VMEM)
SM = pl.BlockSpec(memory_space=pltpu.SMEM)
PAY = A + LANES


def params(mib):
    return pltpu.CompilerParams(vmem_limit_bytes=mib * 1024 * 1024)


def shards(
    features, tissue, partner, dw_kernel, dw_bias, ln_gain, ln_bias, w_up,
    narrowing_projection_kernel, layer_scale, w_embed, embed_bias, attn_v, attn_u, attn_w,
):
    block = (S, R, W, C)
    strip = (S, R, 8, C)
    masked_shapes = (
        jax.ShapeDtypeStruct(block, BF),
        jax.ShapeDtypeStruct(strip, BF),
        jax.ShapeDtypeStruct((N, LANES), F32),
    )
    masked, edge, flags = pl.pallas_call(
        mask_kernel,
        out_shape=masked_shapes,
        in_specs=[HBM, HBM],
        out_specs=(HBM, HBM, HBM),
        scratch_shapes=[pltpu.VMEM(block, BF), pltpu.VMEM((R, S, W), jnp.int32)]
        + [pltpu.VMEM(x.shape, x.dtype) for x in masked_shapes]
        + [pltpu.SemaphoreType.DMA((2 * S + 3,))],
        compiler_params=params(60),
        name="mask",
    )(features, tissue.transpose(1, 0, 2))
    tile = ("z", "xl")
    count = lax.axis_size(tile)
    upward = [(i, i + 1) for i in range(count - 1)]
    downward = [(i + 1, i) for i in range(count - 1)]
    above = lax.ppermute(masked, tile, upward)
    below = lax.ppermute(masked, tile, downward)
    edge_own = lax.ppermute(edge, "section", [(0, 1), (1, 0)])
    every = ("section",) + tile
    edge_above = lax.ppermute(
        edge, every, [(c * count + i, (1 - c) * count + i + 1) for c in range(2) for i in range(count - 1)]
    )
    edge_below = lax.ppermute(
        edge, every, [(c * count + i + 1, (1 - c) * count + i) for c in range(2) for i in range(count - 1)]
    )
    depth = lax.axis_size("z")

    sources = (masked, dw_kernel)
    partial = jax.ShapeDtypeStruct((N, C), F32)
    partial = pl.pallas_call(
        own_kernel,
        out_shape=partial,
        in_specs=[HBM] * len(sources),
        out_specs=HBM,
        scratch_shapes=[pltpu.VMEM(x.shape, x.dtype) for x in sources + (partial,)]
        + [
            pltpu.VMEM((S, 3 * R, PW, C), F32),
            pltpu.VMEM((R, 7, PW, LANES), F32),
            pltpu.SemaphoreType.DMA((3,)),
        ],
        compiler_params=params(64),
        cost_estimate=pl.CostEstimate(flops=10**8, bytes_accessed=2 * 10**6, transcendentals=0),
        name="own_rows",
    )(*sources)
    operands = (
        edge_own, above, edge_above, below, edge_below, dw_kernel, partial, masked, flags, dw_bias, ln_gain,
        ln_bias, layer_scale, embed_bias, attn_w, w_up, narrowing_projection_kernel, w_embed, attn_v, attn_u,
    )
    forward_shapes = (
        jax.ShapeDtypeStruct((depth, S, PAY), F32),
        jax.ShapeDtypeStruct((N, A), BF),
        jax.ShapeDtypeStruct((N, A), BF),
        jax.ShapeDtypeStruct((N, LANES), F32),
        jax.ShapeDtypeStruct((N, AH), BF),
        jax.ShapeDtypeStruct((N, AH), BF),
    )
    payload, embedded, slope, weight, gate_v, gate_u = pl.pallas_call(
        forward_kernel,
        out_shape=forward_shapes,
        in_specs=[HBM] * len(operands),
        out_specs=[HBM] * len(forward_shapes),
        scratch_shapes=[pltpu.VMEM(x.shape, x.dtype) for x in operands + forward_shapes]
        + [
            pltpu.VMEM((S, 3 * R, PW, C), F32),
            pltpu.VMEM((R, 7, PW, LANES), F32),
            pltpu.VMEM((N, C), F32),
            pltpu.VMEM((S, PAY), F32),
            pltpu.SemaphoreType.DMA((28,)),
        ],
        compiler_params=params(60),
        cost_estimate=pl.CostEstimate(flops=2 * 10**9, bytes_accessed=8 * 10**6, transcendentals=10**6),
        name="forward",
    )(*operands)
    gate_term = pl.pallas_call(
        slope_kernel,
        out_shape=jax.ShapeDtypeStruct((N, C), F32),
        in_specs=[VM] * 3 + [HBM] * 3,
        out_specs=VM,
        scratch_shapes=[
            pltpu.VMEM((C, A), BF),
            pltpu.VMEM((A, AH), BF),
            pltpu.VMEM((A, AH), BF),
            pltpu.SemaphoreType.DMA((3,)),
        ],
        compiler_params=params(24),
        cost_estimate=pl.CostEstimate(flops=10**9, bytes_accessed=4 * 10**6, transcendentals=0),
        name="gate_term",
    )(gate_v, gate_u, slope, w_embed, attn_v, attn_u)

    plane = ("section", "xl", "set")
    received = lax.all_to_all(payload, "z", 0, 0, tiled=True)
    payload = pl.pallas_call(
        sum_kernel,
        out_shape=jax.ShapeDtypeStruct((lax.axis_size(plane), S, PAY), F32),
        in_specs=[VM, HBM],
        out_specs=VM,
        compiler_params=params(24),
        name="add_up",
    )(received, gate_term)
    received = lax.all_to_all(payload, plane, 0, 0, tiled=True)
    slides = partner.shape[0]
    return pl.pallas_call(
        final_kernel,
        out_shape=(
            jax.ShapeDtypeStruct((S,), F32),
            jax.ShapeDtypeStruct((S, A), F32),
            jax.ShapeDtypeStruct((S, R, W, C), BF),
        ),
        in_specs=[VM] * 6 + [HBM],
        out_specs=(SM, VM, VM),
        scratch_shapes=[
            pltpu.VMEM((slides, PAY), F32),
            pltpu.VMEM((C, A), BF),
            pltpu.SemaphoreType.DMA(()),
        ],
        compiler_params=params(24),
        name="final",
    )(received, partner.reshape(1, slides), embedded, slope, weight, gate_term, w_embed)


def solution(mesh):
    section, tile, groups = mesh.devices.shape
    fine = Mesh(
        mesh.devices.reshape(section, tile // 2, 2, groups), ("section", "z", "xl", "set")
    )
    tiles = ("z", "xl")
    placed = (P("set", tiles, "section", None), P("set", tiles, "section")) + (P(),) * 13
    return jax.shard_map(
        shards,
        mesh=fine,
        in_specs=placed,
        out_specs=(P("set"), P("set", None), P("set", tiles, "section", None)),
        check_vma=False,
    )
```

```python
import jax
import jax.numpy as jnp
from jax import lax
from jax.experimental import pallas as pl
from jax.experimental.pallas import tpu as pltpu
from jax.sharding import Mesh
from jax.sharding import PartitionSpec as P

C = 384
HID = 1536
A = 1024
AH = 256
S = 2
R = 3
W = 64
N = S * R * W
PW = W + 8
LANES = 128
HALF = S * R * W // S
INV_T = 10.0
SCALE = 65536.0
RSQRT2 = 0.7071067811865476
RSQRT2PI = 0.3989422804014327
NT = (((1,), (1,)), ((), ()))
HI = lax.Precision.HIGHEST
F32 = jnp.float32
BF = jnp.bfloat16


def copies_between(pairs, sems, first=0):
    return [
        pltpu.make_async_copy(src, dst, sems.at[first + i]) for i, (src, dst) in enumerate(pairs)
    ]


def mask_kernel(
    features_hbm, tissue_hbm, masked_hbm, edge_hbm, flags_hbm,
    features, tissue, masked, edge, flags, sems,
):
    first_in = pltpu.make_async_copy(tissue_hbm, tissue, sems.at[2 * S])
    arrive = copies_between([(features_hbm.at[s], features.at[s]) for s in range(S)], sems)
    leave = copies_between([(masked.at[s], masked_hbm.at[s]) for s in range(S)], sems, S)
    last_out = copies_between([(edge, edge_hbm), (flags, flags_hbm)], sems, 2 * S + 1)
    first_in.start()
    for c in arrive:
        c.start()
    side = lax.axis_index("section")
    place = lax.broadcasted_iota(jnp.int32, (8, C), 0)
    first = jnp.where((place < 3) & (side == 1), 1.0, 0.0)
    last = jnp.where((place >= 5) & (side == 0), 1.0, 0.0)
    first_in.wait()
    rows = [tissue[r, s : s + 1, :].astype(F32) for s in range(S) for r in range(R)]
    turned = jnp.concatenate(rows + rows[:2], axis=0).T
    for s in range(S):
        arrive[s].wait()
        for r in range(R):
            i = s * R + r
            here = jnp.broadcast_to(turned[:, i : i + 1], (W, LANES))
            flags[i * W : i * W + W, :] = here
            wide = jnp.concatenate([here] * (C // LANES), axis=1)
            values = features[s, r].astype(F32) * wide
            masked[s, r] = values.astype(BF)
            edge[s, r] = (values[:8] * first + values[W - 8 :] * last).astype(BF)
        leave[s].start()
    for c in last_out:
        c.start()
    for c in leave + last_out:
        c.wait()


def fill(grid_ref, at, block, edge):
    for s in range(S):
        for r in range(R):
            if block is not None:
                grid_ref[s, at + r, 0:W, :] = block[s, r].astype(F32)
            if edge is not None:
                grid_ref[s, at + r, W:PW, :] = edge[s, r].astype(F32)


def convolve(grid_ref, acc_ref, conv_ref, dw_k, inner, outer, seed):
    def conv_lane(step, carry):
        s = step // (C // LANES)
        lane = pl.multiple_of(lax.rem(step, C // LANES) * LANES, LANES)
        for col in range(PW // 8):
            cols = slice(col * 8, col * 8 + 8)
            places = inner if col < W // 8 else outer
            rows = [grid_ref[s, r, cols, pl.ds(lane, LANES)] for r in places]
            for b in range(7):
                sums = [None] * R
                for a in range(7):
                    pairs = [(places.index(a + i), i) for i in range(R) if a + i in places]
                    if not pairs:
                        continue
                    k = dw_k[a, b, pl.ds(lane, LANES)].reshape(1, LANES)
                    for row, i in pairs:
                        term = rows[row] * k
                        sums[i] = term if sums[i] is None else sums[i] + term
                for i in range(R):
                    empty = sums[i] is None
                    acc_ref[i, b, cols, :] = jnp.zeros((8, LANES), F32) if empty else sums[i]
        for i in range(R):
            total = acc_ref[i, 3]
            for b in (0, 1, 2, 4, 5, 6):
                total = total + pltpu.roll(acc_ref[i, b], (3 - b) % PW, 0)
            at = pl.multiple_of(s * R * W + i * W, W)
            where = (pl.ds(at, W), pl.ds(lane, LANES))
            total = total[0:W]
            conv_ref[where] = total if seed is None else total + seed[where]
        return carry

    lax.fori_loop(0, S * (C // LANES), conv_lane, 0)


def own_kernel(
    own_hbm, dw_k_hbm, partial_hbm, own, dw_k, partial, grid_ref, acc_ref, sems
):
    arrive = copies_between(((own_hbm, own), (dw_k_hbm, dw_k)), sems)
    for c in arrive:
        c.start()
    for c in arrive:
        c.wait()
    fill(grid_ref, R, own, None)
    convolve(grid_ref, acc_ref, partial, dw_k, (3, 4, 5), (), None)
    leave = pltpu.make_async_copy(partial, partial_hbm, sems.at[2])
    leave.start()
    leave.wait()


def forward_kernel(
    edge_own_hbm, above_hbm, edge_above_hbm, below_hbm, edge_below_hbm, dw_k_hbm, partial_hbm, own_hbm,
    flags_hbm, dw_b_hbm, ln_g_hbm, ln_b_hbm, scale_hbm, e_bias_hbm, a_w_hbm,
    up_hbm, down_hbm, emb_hbm, v_hbm, u_hbm,
    payload_hbm, embedded_hbm, slope_hbm, weight_hbm, gate_v_hbm, gate_u_hbm,
    edge_own, above, edge_above, below, edge_below, dw_k, partial, own,
    flags, dw_b, ln_g, ln_b, scale, e_bias, a_w, up, down, emb, att_v, att_u,
    payload, embedded_out, slope_out, weight_out, gate_v_out, gate_u_out,
    grid_ref, acc_ref, conv_ref, sums_ref, sems,
):
    blocks = copies_between(
        (
            (above_hbm, above), (edge_above_hbm, edge_above), (below_hbm, below),
            (edge_below_hbm, edge_below), (edge_own_hbm, edge_own), (dw_k_hbm, dw_k),
            (partial_hbm, partial),
        ),
        sems,
    )
    small = copies_between(
        (
            (own_hbm, own), (dw_b_hbm, dw_b), (ln_g_hbm, ln_g), (ln_b_hbm, ln_b),
            (scale_hbm, scale), (e_bias_hbm, e_bias), (a_w_hbm, a_w), (flags_hbm, flags),
        ),
        sems,
        7,
    )
    copies = copies_between(
        ((up_hbm, up), (down_hbm, down), (emb_hbm, emb), (v_hbm, att_v), (u_hbm, att_u)), sems, 15
    )
    embed_step = 512
    halves = [slice(h, h + embed_step) for h in range(0, A, embed_step)]
    early = copies_between(
        [
            (vm.at[:, cols], hbm.at[:, cols])
            for cols in halves
            for vm, hbm in ((embedded_out, embedded_hbm), (slope_out, slope_hbm))
        ],
        sems,
        20,
    )
    results = copies_between(
        (
            (weight_out, weight_hbm), (payload, payload_hbm), (gate_v_out, gate_v_hbm),
            (gate_u_out, gate_u_hbm),
        ),
        sems,
        24,
    )
    for c in blocks:
        c.start()
    for c in blocks:
        c.wait()
    for c in small + copies:
        c.start()
    fill(grid_ref, 0, above, edge_above)
    fill(grid_ref, R, None, edge_own)
    fill(grid_ref, 2 * R, below, edge_below)
    convolve(
        grid_ref, acc_ref, conv_ref, dw_k, (0, 1, 2, 6, 7, 8), tuple(range(3 * R)), partial
    )
    for c in small:
        c.wait()
    conv = conv_ref[...] + dw_b[...].reshape(1, -1)
    centre = jnp.mean(conv, axis=-1, keepdims=True)
    moved = conv - centre
    spread = jnp.mean(moved * moved, axis=-1, keepdims=True)
    normed = (moved * lax.rsqrt(spread + 1e-06) * ln_g[...].reshape(1, -1) + ln_b[...].reshape(1, -1)).astype(BF)
    copies[0].wait()
    copies[1].wait()
    branch = jnp.zeros((N, C), F32)
    step = 768
    for h in range(0, HID, step):
        raised = jnp.dot(normed, up[:, h : h + step], preferred_element_type=F32)
        hidden = (0.5 * raised * (1.0 + lax.erf(raised * RSQRT2))).astype(BF)
        branch = branch + jnp.dot(hidden, down[h : h + step, :], preferred_element_type=F32)
    tissue = flags[...]
    wide = jnp.concatenate([tissue] * (C // LANES), axis=1)
    masked = own[...].reshape(N, C).astype(F32)
    trunk = ((masked + scale[...].reshape(1, -1) * branch) * wide).astype(BF)
    copies[2].wait()
    copies[3].wait()
    copies[4].wait()
    logits_v = jnp.zeros((N, AH), F32)
    logits_u = jnp.zeros((N, AH), F32)
    for h, cols in enumerate(halves):
        pre = jnp.dot(trunk, emb[:, cols], preferred_element_type=F32) + e_bias[cols].reshape(1, -1)
        cdf = 0.5 * (1.0 + lax.erf(pre * RSQRT2))
        slope = cdf + pre * (RSQRT2PI * jnp.exp(-0.5 * pre * pre))
        out = (pre * cdf).astype(BF)
        embedded_out[:, cols] = out
        slope_out[:, cols] = slope.astype(BF)
        early[2 * h].start()
        early[2 * h + 1].start()
        logits_v = logits_v + jnp.dot(out, att_v[cols, :], preferred_element_type=F32)
        logits_u = logits_u + jnp.dot(out, att_u[cols, :], preferred_element_type=F32)
    tangent = jnp.tanh(logits_v)
    opening = jax.nn.sigmoid(logits_u)
    aw = a_w[...].reshape(1, -1)
    product = tangent * opening * aw
    scores = jnp.sum(product, axis=-1, keepdims=True)
    weight = tissue * jnp.exp(scores)
    weight_out[...] = weight
    results[0].start()
    for s in range(S):
        rows = slice(s * HALF, s * HALF + HALF)
        w_here = weight[rows, :]
        for k in range(A // LANES):
            cols = slice(k * LANES, k * LANES + LANES)
            part = jnp.sum(w_here * embedded_out[rows, cols].astype(F32), axis=0, keepdims=True)
            sums_ref[s : s + 1, cols] = part
        sums_ref[s : s + 1, A:] = jnp.sum(w_here, axis=0, keepdims=True)
    payload[...] = jnp.broadcast_to(sums_ref[...][None], payload.shape)
    results[1].start()
    gate_v_out[...] = (aw * opening * (1.0 - tangent * tangent)).astype(BF)
    gate_u_out[...] = (product * (1.0 - opening)).astype(BF)
    results[2].start()
    results[3].start()
    for c in early + results:
        c.wait()


def sum_kernel(received, payload):
    total = jnp.sum(received[...], axis=0)
    payload[...] = jnp.broadcast_to(total[None], payload.shape)


def final_kernel(
    received, partner, embedded_hbm, weight_hbm, gate_v_hbm, gate_u_hbm, slope_hbm, v_hbm, u_hbm,
    emb_hbm, loss_out, vector_out, grad_out,
    embedded, weight, gate_v, gate_u, slope, att_v, att_u, emb, sums_ref, scaled_v, scaled_u, sems,
):
    fetch = copies_between(
        (
            (embedded_hbm, embedded), (weight_hbm, weight), (gate_v_hbm, gate_v),
            (gate_u_hbm, gate_u), (slope_hbm, slope), (v_hbm, att_v), (u_hbm, att_u),
            (emb_hbm, emb),
        ),
        sems,
    )
    for c in fetch:
        c.start()
    position = lax.axis_index("set")
    slides = sums_ref.shape[0]
    groups = slides // S
    for g in range(groups):
        gathered = received[g]
        for part in range(1, received.shape[0] // groups):
            gathered = gathered + received[part * groups + g]
        sums_ref[g * S : g * S + S, :] = gathered
    totals = sums_ref[:, A:]
    pooled = sums_ref[:, :A] / totals[:, :1]
    radius = jnp.sqrt(jnp.sum(pooled * pooled, axis=-1, keepdims=True) + 1e-06)
    vector = pooled / radius
    table = (
        lax.dot_general(vector, vector, NT, precision=HI, preferred_element_type=F32) * INV_T
    )
    row = lax.broadcasted_iota(jnp.int32, (slides, slides), 0)
    col = lax.broadcasted_iota(jnp.int32, (slides, slides), 1)
    positive = jnp.where(row == partner[...], 1.0, 0.0)
    exps = jnp.where(row != col, jnp.exp(table), 0.0)
    normaliser = jnp.sum(exps, axis=-1, keepdims=True)
    losses = jnp.log(normaliser) - jnp.sum(positive * table, axis=-1, keepdims=True)
    coefficients = exps / normaliser - positive
    both = coefficients + coefficients.T
    embed_grad = jnp.dot(both, vector, precision=HI, preferred_element_type=F32) * INV_T
    projection = jnp.sum(pooled * embed_grad, axis=-1, keepdims=True)
    pooled_grad = SCALE * (
        embed_grad / radius - pooled * (projection / (radius * radius * radius))
    )
    dots = jnp.sum(pooled_grad * pooled, axis=-1, keepdims=True)
    index = lax.broadcasted_iota(jnp.int32, (slides, 1), 0)
    leading = []
    for c in fetch[:4]:
        c.wait()
    for s in range(S):
        mine = index == position * S + s

        def pick(values):
            return jnp.sum(jnp.where(mine, values, 0.0), axis=0, keepdims=True)

        vector_out[s : s + 1, :] = pick(vector)
        loss_out[s] = jnp.sum(jnp.where(mine, losses, 0.0))
        grad = pick(pooled_grad)
        dot = pick(dots)
        total = pick(totals)
        rows = slice(s * HALF, s * HALF + HALF)
        aligned = jnp.sum(embedded[rows, :].astype(F32) * grad, axis=-1, keepdims=True)
        share = weight[rows, :] / total
        score = share * (aligned - dot)
        leading.append((share, grad))
        score = jnp.concatenate([score] * (AH // LANES), axis=1)
        scaled_v[rows, :] = (score * gate_v[rows, :].astype(F32)).astype(BF)
        scaled_u[rows, :] = (score * gate_u[rows, :].astype(F32)).astype(BF)
    for c in fetch[4:]:
        c.wait()
    fresh = jnp.zeros((N, C), F32)
    step = 512
    for h in range(0, A, step):
        cols = slice(h, h + step)
        back = lax.dot_general(scaled_v[...], att_v[cols, :], NT, preferred_element_type=F32)
        back = back + lax.dot_general(scaled_u[...], att_u[cols, :], NT, preferred_element_type=F32)
        lead = jnp.concatenate(
            [
                jnp.concatenate([share] * (step // LANES), axis=1) * grad[:, cols]
                for share, grad in leading
            ],
            axis=0,
        )
        moved = ((lead + back) * slope[:, cols].astype(F32)).astype(BF)
        fresh = fresh + lax.dot_general(moved, emb[:, cols], NT, preferred_element_type=F32)
    grad_out[...] = fresh.astype(BF).reshape(S, R, W, C)


HBM = pl.BlockSpec(memory_space=pltpu.HBM)
VM = pl.BlockSpec(memory_space=pltpu.VMEM)
SM = pl.BlockSpec(memory_space=pltpu.SMEM)
PAY = A + LANES


def params(mib):
    return pltpu.CompilerParams(vmem_limit_bytes=mib * 1024 * 1024)


def shards(
    features, tissue, partner, dw_kernel, dw_bias, ln_gain, ln_bias, w_up,
    narrowing_projection_kernel, layer_scale, w_embed, embed_bias, attn_v, attn_u, attn_w,
):
    block = (S, R, W, C)
    strip = (S, R, 8, C)
    masked_shapes = (
        jax.ShapeDtypeStruct(block, BF),
        jax.ShapeDtypeStruct(strip, BF),
        jax.ShapeDtypeStruct((N, LANES), F32),
    )
    masked, edge, flags = pl.pallas_call(
        mask_kernel,
        out_shape=masked_shapes,
        in_specs=[HBM, HBM],
        out_specs=(HBM, HBM, HBM),
        scratch_shapes=[pltpu.VMEM(block, BF), pltpu.VMEM((R, S, W), jnp.int32)]
        + [pltpu.VMEM(x.shape, x.dtype) for x in masked_shapes]
        + [pltpu.SemaphoreType.DMA((2 * S + 3,))],
        compiler_params=params(60),
        name="mask",
    )(features, tissue.transpose(1, 0, 2))
    tile = ("z", "xl")
    count = lax.axis_size(tile)
    upward = [(i, i + 1) for i in range(count - 1)]
    downward = [(i + 1, i) for i in range(count - 1)]
    above = lax.ppermute(masked, tile, upward)
    below = lax.ppermute(masked, tile, downward)
    edge_own = lax.ppermute(edge, "section", [(0, 1), (1, 0)])
    every = ("section",) + tile
    edge_above = lax.ppermute(
        edge, every, [(c * count + i, (1 - c) * count + i + 1) for c in range(2) for i in range(count - 1)]
    )
    edge_below = lax.ppermute(
        edge, every, [(c * count + i + 1, (1 - c) * count + i) for c in range(2) for i in range(count - 1)]
    )
    depth = lax.axis_size("z")

    sources = (masked, dw_kernel)
    partial = jax.ShapeDtypeStruct((N, C), F32)
    partial = pl.pallas_call(
        own_kernel,
        out_shape=partial,
        in_specs=[HBM] * len(sources),
        out_specs=HBM,
        scratch_shapes=[pltpu.VMEM(x.shape, x.dtype) for x in sources + (partial,)]
        + [
            pltpu.VMEM((S, 3 * R, PW, C), F32),
            pltpu.VMEM((R, 7, PW, LANES), F32),
            pltpu.SemaphoreType.DMA((3,)),
        ],
        compiler_params=params(64),
        cost_estimate=pl.CostEstimate(flops=10**8, bytes_accessed=2 * 10**6, transcendentals=0),
        name="own_rows",
    )(*sources)
    operands = (
        edge_own, above, edge_above, below, edge_below, dw_kernel, partial, masked, flags, dw_bias, ln_gain,
        ln_bias, layer_scale, embed_bias, attn_w, w_up, narrowing_projection_kernel, w_embed, attn_v, attn_u,
    )
    forward_shapes = (
        jax.ShapeDtypeStruct((depth, S, PAY), F32),
        jax.ShapeDtypeStruct((N, A), BF),
        jax.ShapeDtypeStruct((N, A), BF),
        jax.ShapeDtypeStruct((N, LANES), F32),
        jax.ShapeDtypeStruct((N, AH), BF),
        jax.ShapeDtypeStruct((N, AH), BF),
    )
    payload, embedded, slope, weight, gate_v, gate_u = pl.pallas_call(
        forward_kernel,
        out_shape=forward_shapes,
        in_specs=[HBM] * len(operands),
        out_specs=[HBM] * len(forward_shapes),
        scratch_shapes=[pltpu.VMEM(x.shape, x.dtype) for x in operands + forward_shapes]
        + [
            pltpu.VMEM((S, 3 * R, PW, C), F32),
            pltpu.VMEM((R, 7, PW, LANES), F32),
            pltpu.VMEM((N, C), F32),
            pltpu.VMEM((S, PAY), F32),
            pltpu.SemaphoreType.DMA((28,)),
        ],
        compiler_params=params(60),
        cost_estimate=pl.CostEstimate(flops=2 * 10**9, bytes_accessed=8 * 10**6, transcendentals=10**6),
        name="forward",
    )(*operands)
    plane = ("section", "xl", "set")
    received = lax.all_to_all(payload, "z", 0, 0, tiled=True)
    payload = pl.pallas_call(
        sum_kernel,
        out_shape=jax.ShapeDtypeStruct((lax.axis_size(plane), S, PAY), F32),
        in_specs=[VM],
        out_specs=VM,
        compiler_params=params(24),
        name="add_up",
    )(received)
    received = lax.all_to_all(payload, plane, 0, 0, tiled=True)
    slides = partner.shape[0]
    kept = (embedded, weight, gate_v, gate_u, slope, attn_v, attn_u, w_embed)
    return pl.pallas_call(
        final_kernel,
        out_shape=(
            jax.ShapeDtypeStruct((S,), F32),
            jax.ShapeDtypeStruct((S, A), F32),
            jax.ShapeDtypeStruct((S, R, W, C), BF),
        ),
        in_specs=[VM, VM] + [HBM] * len(kept),
        out_specs=(SM, VM, VM),
        scratch_shapes=[pltpu.VMEM(x.shape, x.dtype) for x in kept]
        + [
            pltpu.VMEM((slides, PAY), F32),
            pltpu.VMEM((N, AH), BF),
            pltpu.VMEM((N, AH), BF),
            pltpu.SemaphoreType.DMA((len(kept),)),
        ],
        compiler_params=params(53),
        name="final",
    )(received, partner.reshape(1, slides), *kept)


def solution(mesh):
    section, tile, groups = mesh.devices.shape
    fine = Mesh(
        mesh.devices.reshape(section, tile // 2, 2, groups), ("section", "z", "xl", "set")
    )
    tiles = ("z", "xl")
    placed = (P("set", tiles, "section", None), P("set", tiles, "section")) + (P(),) * 13
    return jax.shard_map(
        shards,
        mesh=fine,
        in_specs=placed,
        out_specs=(P("set"), P("set", None), P("set", tiles, "section", None)),
        check_vma=False,
    )
```

```python
import jax
import jax.numpy as jnp
from jax import lax
from jax.experimental import pallas as pl
from jax.experimental.pallas import tpu as pltpu
from jax.sharding import Mesh
from jax.sharding import PartitionSpec as P

C = 384
HID = 1536
A = 1024
AH = 256
S = 2
R = 3
W = 64
N = S * R * W
PW = W + 8
LANES = 128
HALF = S * R * W // S
INV_T = 10.0
SCALE = 65536.0
RSQRT2 = 0.7071067811865476
RSQRT2PI = 0.3989422804014327
NT = (((1,), (1,)), ((), ()))
HI = lax.Precision.HIGHEST
F32 = jnp.float32
BF = jnp.bfloat16


def copies_between(pairs, sems, first=0):
    return [
        pltpu.make_async_copy(src, dst, sems.at[first + i]) for i, (src, dst) in enumerate(pairs)
    ]


def mask_kernel(
    features_hbm, tissue_hbm, masked_hbm, edge_hbm, flags_hbm,
    features, tissue, masked, edge, flags, sems,
):
    first_in = pltpu.make_async_copy(tissue_hbm, tissue, sems.at[2 * S])
    arrive = copies_between([(features_hbm.at[s], features.at[s]) for s in range(S)], sems)
    leave = copies_between([(masked.at[s], masked_hbm.at[s]) for s in range(S)], sems, S)
    last_out = copies_between([(edge, edge_hbm), (flags, flags_hbm)], sems, 2 * S + 1)
    first_in.start()
    for c in arrive:
        c.start()
    side = lax.axis_index("section")
    place = lax.broadcasted_iota(jnp.int32, (8, C), 0)
    first = jnp.where((place < 3) & (side == 1), 1.0, 0.0)
    last = jnp.where((place >= 5) & (side == 0), 1.0, 0.0)
    first_in.wait()
    rows = [tissue[r, s : s + 1, :].astype(F32) for s in range(S) for r in range(R)]
    turned = jnp.concatenate(rows + rows[:2], axis=0).T
    for s in range(S):
        arrive[s].wait()
        for r in range(R):
            i = s * R + r
            here = jnp.broadcast_to(turned[:, i : i + 1], (W, LANES))
            flags[i * W : i * W + W, :] = here
            wide = jnp.concatenate([here] * (C // LANES), axis=1)
            values = features[s, r].astype(F32) * wide
            masked[s, r] = values.astype(BF)
            edge[s, r] = (values[:8] * first + values[W - 8 :] * last).astype(BF)
        leave[s].start()
    for c in last_out:
        c.start()
    for c in leave + last_out:
        c.wait()


def fill(grid_ref, at, block, edge):
    for s in range(S):
        for r in range(R):
            if block is not None:
                grid_ref[s, at + r, 0:W, :] = block[s, r].astype(F32)
            if edge is not None:
                grid_ref[s, at + r, W:PW, :] = edge[s, r].astype(F32)


def convolve(grid_ref, acc_ref, conv_ref, dw_k, inner, outer, seed):
    def conv_lane(step, carry):
        s = step // (C // LANES)
        lane = pl.multiple_of(lax.rem(step, C // LANES) * LANES, LANES)
        for col in range(PW // 8):
            cols = slice(col * 8, col * 8 + 8)
            places = inner if col < W // 8 else outer
            rows = [grid_ref[s, r, cols, pl.ds(lane, LANES)] for r in places]
            for b in range(7):
                sums = [None] * R
                for a in range(7):
                    pairs = [(places.index(a + i), i) for i in range(R) if a + i in places]
                    if not pairs:
                        continue
                    k = dw_k[a, b, pl.ds(lane, LANES)].reshape(1, LANES)
                    for row, i in pairs:
                        term = rows[row] * k
                        sums[i] = term if sums[i] is None else sums[i] + term
                for i in range(R):
                    empty = sums[i] is None
                    acc_ref[i, b, cols, :] = jnp.zeros((8, LANES), F32) if empty else sums[i]
        for i in range(R):
            total = acc_ref[i, 3]
            for b in (0, 1, 2, 4, 5, 6):
                total = total + pltpu.roll(acc_ref[i, b], (3 - b) % PW, 0)
            at = pl.multiple_of(s * R * W + i * W, W)
            where = (pl.ds(at, W), pl.ds(lane, LANES))
            total = total[0:W]
            conv_ref[where] = total if seed is None else total + seed[where]
        return carry

    lax.fori_loop(0, S * (C // LANES), conv_lane, 0)


def own_kernel(
    own_hbm, dw_k_hbm, partial_hbm, own, dw_k, partial, grid_ref, acc_ref, sems
):
    arrive = copies_between(((own_hbm, own), (dw_k_hbm, dw_k)), sems)
    for c in arrive:
        c.start()
    for c in arrive:
        c.wait()
    fill(grid_ref, R, own, None)
    convolve(grid_ref, acc_ref, partial, dw_k, (3, 4, 5), (), None)
    leave = pltpu.make_async_copy(partial, partial_hbm, sems.at[2])
    leave.start()
    leave.wait()


def forward_kernel(
    edge_own_hbm, near_hbm, edge_near_hbm, far_hbm, edge_far_hbm, dw_k_hbm, partial_hbm, own_hbm,
    flags_hbm, dw_b_hbm, ln_g_hbm, ln_b_hbm, scale_hbm, e_bias_hbm, a_w_hbm,
    up_hbm, down_hbm, emb_hbm, v_hbm, u_hbm,
    payload_hbm, embedded_hbm, slope_hbm, weight_hbm, gate_v_hbm, gate_u_hbm,
    edge_own, near, edge_near, far, edge_far, dw_k, partial, own,
    flags, dw_b, ln_g, ln_b, scale, e_bias, a_w, up, down, emb, att_v, att_u,
    payload, embedded_out, slope_out, weight_out, gate_v_out, gate_u_out,
    grid_ref, acc_ref, conv_ref, sums_ref, sems,
):
    blocks = copies_between(
        (
            (near_hbm, near), (edge_near_hbm, edge_near), (far_hbm, far),
            (edge_far_hbm, edge_far), (edge_own_hbm, edge_own), (dw_k_hbm, dw_k),
            (partial_hbm, partial),
        ),
        sems,
    )
    small = copies_between(
        (
            (own_hbm, own), (dw_b_hbm, dw_b), (ln_g_hbm, ln_g), (ln_b_hbm, ln_b),
            (scale_hbm, scale), (e_bias_hbm, e_bias), (a_w_hbm, a_w), (flags_hbm, flags),
        ),
        sems,
        7,
    )
    copies = copies_between(
        ((up_hbm, up), (down_hbm, down), (emb_hbm, emb), (v_hbm, att_v), (u_hbm, att_u)), sems, 15
    )
    embed_step = 512
    halves = [slice(h, h + embed_step) for h in range(0, A, embed_step)]
    early = copies_between(
        [
            (vm.at[:, cols], hbm.at[:, cols])
            for cols in halves
            for vm, hbm in ((embedded_out, embedded_hbm), (slope_out, slope_hbm))
        ],
        sems,
        20,
    )
    results = copies_between(
        (
            (weight_out, weight_hbm), (payload, payload_hbm), (gate_v_out, gate_v_hbm),
            (gate_u_out, gate_u_hbm),
        ),
        sems,
        24,
    )
    for c in blocks:
        c.start()
    for c in blocks:
        c.wait()
    for c in small + copies:
        c.start()
    odd = lax.axis_index("xl") == 1
    fill(grid_ref, jnp.where(odd, 2 * R, 0), far, edge_far)
    fill(grid_ref, R, None, edge_own)
    fill(grid_ref, jnp.where(odd, 0, 2 * R), near, edge_near)
    convolve(
        grid_ref, acc_ref, conv_ref, dw_k, (0, 1, 2, 6, 7, 8), tuple(range(3 * R)), partial
    )
    for c in small:
        c.wait()
    conv = conv_ref[...] + dw_b[...].reshape(1, -1)
    centre = jnp.mean(conv, axis=-1, keepdims=True)
    moved = conv - centre
    spread = jnp.mean(moved * moved, axis=-1, keepdims=True)
    normed = (moved * lax.rsqrt(spread + 1e-06) * ln_g[...].reshape(1, -1) + ln_b[...].reshape(1, -1)).astype(BF)
    copies[0].wait()
    copies[1].wait()
    branch = jnp.zeros((N, C), F32)
    step = 768
    for h in range(0, HID, step):
        raised = jnp.dot(normed, up[:, h : h + step], preferred_element_type=F32)
        hidden = (0.5 * raised * (1.0 + lax.erf(raised * RSQRT2))).astype(BF)
        branch = branch + jnp.dot(hidden, down[h : h + step, :], preferred_element_type=F32)
    tissue = flags[...]
    wide = jnp.concatenate([tissue] * (C // LANES), axis=1)
    masked = own[...].reshape(N, C).astype(F32)
    trunk = ((masked + scale[...].reshape(1, -1) * branch) * wide).astype(BF)
    copies[2].wait()
    copies[3].wait()
    copies[4].wait()
    logits_v = jnp.zeros((N, AH), F32)
    logits_u = jnp.zeros((N, AH), F32)
    for h, cols in enumerate(halves):
        pre = jnp.dot(trunk, emb[:, cols], preferred_element_type=F32) + e_bias[cols].reshape(1, -1)
        cdf = 0.5 * (1.0 + lax.erf(pre * RSQRT2))
        slope = cdf + pre * (RSQRT2PI * jnp.exp(-0.5 * pre * pre))
        out = (pre * cdf).astype(BF)
        embedded_out[:, cols] = out
        slope_out[:, cols] = slope.astype(BF)
        early[2 * h].start()
        early[2 * h + 1].start()
        logits_v = logits_v + jnp.dot(out, att_v[cols, :], preferred_element_type=F32)
        logits_u = logits_u + jnp.dot(out, att_u[cols, :], preferred_element_type=F32)
    tangent = jnp.tanh(logits_v)
    opening = jax.nn.sigmoid(logits_u)
    aw = a_w[...].reshape(1, -1)
    product = tangent * opening * aw
    scores = jnp.sum(product, axis=-1, keepdims=True)
    weight = tissue * jnp.exp(scores)
    weight_out[...] = weight
    results[0].start()
    for s in range(S):
        rows = slice(s * HALF, s * HALF + HALF)
        w_here = weight[rows, :]
        for k in range(A // LANES):
            cols = slice(k * LANES, k * LANES + LANES)
            part = jnp.sum(w_here * embedded_out[rows, cols].astype(F32), axis=0, keepdims=True)
            sums_ref[s : s + 1, cols] = part
        sums_ref[s : s + 1, A:] = jnp.sum(w_here, axis=0, keepdims=True)
    payload[...] = jnp.broadcast_to(sums_ref[...][None], payload.shape)
    results[1].start()
    gate_v_out[...] = (aw * opening * (1.0 - tangent * tangent)).astype(BF)
    gate_u_out[...] = (product * (1.0 - opening)).astype(BF)
    results[2].start()
    results[3].start()
    for c in early + results:
        c.wait()


def slope_kernel(
    gate_v, gate_u, slope, emb_hbm, v_hbm, u_hbm, out, emb, att_v, att_u, sems
):
    copies = [
        pltpu.make_async_copy(src, dst, sems.at[i])
        for i, (src, dst) in enumerate(((v_hbm, att_v), (u_hbm, att_u), (emb_hbm, emb)))
    ]
    for c in copies:
        c.start()
    for c in copies:
        c.wait()
    total = jnp.zeros((N, C), F32)
    step = 256
    for h in range(0, A, step):
        cols = slice(h, h + step)
        back = lax.dot_general(gate_v[...], att_v[cols, :], NT, preferred_element_type=F32)
        back = back + lax.dot_general(gate_u[...], att_u[cols, :], NT, preferred_element_type=F32)
        back = (back * slope[:, cols].astype(F32)).astype(BF)
        total = total + lax.dot_general(back, emb[:, cols], NT, preferred_element_type=F32)
    out[...] = total


def sum_kernel(received, ahead, payload):
    total = jnp.sum(received[...], axis=0)
    payload[...] = jnp.broadcast_to(total[None], payload.shape)


def final_kernel(
    received, partner, embedded, slope, weight, gate_term, emb_hbm,
    loss_out, vector_out, grad_out, sums_ref, emb, sem,
):
    fetch = pltpu.make_async_copy(emb_hbm, emb, sem)
    fetch.start()
    position = lax.axis_index("set")
    slides = sums_ref.shape[0]
    groups = slides // S
    for g in range(groups):
        gathered = received[g]
        for part in range(1, received.shape[0] // groups):
            gathered = gathered + received[part * groups + g]
        sums_ref[g * S : g * S + S, :] = gathered
    totals = sums_ref[:, A:]
    pooled = sums_ref[:, :A] / totals[:, :1]
    radius = jnp.sqrt(jnp.sum(pooled * pooled, axis=-1, keepdims=True) + 1e-06)
    vector = pooled / radius
    table = (
        lax.dot_general(vector, vector, NT, precision=HI, preferred_element_type=F32) * INV_T
    )
    row = lax.broadcasted_iota(jnp.int32, (slides, slides), 0)
    col = lax.broadcasted_iota(jnp.int32, (slides, slides), 1)
    positive = jnp.where(row == partner[...], 1.0, 0.0)
    exps = jnp.where(row != col, jnp.exp(table), 0.0)
    normaliser = jnp.sum(exps, axis=-1, keepdims=True)
    losses = jnp.log(normaliser) - jnp.sum(positive * table, axis=-1, keepdims=True)
    coefficients = exps / normaliser - positive
    both = coefficients + coefficients.T
    embed_grad = jnp.dot(both, vector, precision=HI, preferred_element_type=F32) * INV_T
    projection = jnp.sum(pooled * embed_grad, axis=-1, keepdims=True)
    pooled_grad = SCALE * (
        embed_grad / radius - pooled * (projection / (radius * radius * radius))
    )
    dots = jnp.sum(pooled_grad * pooled, axis=-1, keepdims=True)
    index = lax.broadcasted_iota(jnp.int32, (slides, 1), 0)
    fetch.wait()
    for s in range(S):
        mine = index == position * S + s

        def pick(values):
            return jnp.sum(jnp.where(mine, values, 0.0), axis=0, keepdims=True)

        vector_out[s : s + 1, :] = pick(vector)
        loss_out[s] = jnp.sum(jnp.where(mine, losses, 0.0))
        grad = pick(pooled_grad)
        dot = pick(dots)
        total = pick(totals)
        rows = slice(s * HALF, s * HALF + HALF)
        aligned = jnp.sum(embedded[rows, :].astype(F32) * grad, axis=-1, keepdims=True)
        share = weight[rows, :] / total
        score = share * (aligned - dot)
        moved = (slope[rows, :].astype(F32) * grad).astype(BF)
        back = lax.dot_general(moved, emb[...], NT, preferred_element_type=F32)
        share = jnp.concatenate([share] * (C // LANES), axis=1)
        score = jnp.concatenate([score] * (C // LANES), axis=1)
        fresh = share * back + score * gate_term[rows, :]
        grad_out[s] = fresh.astype(BF).reshape(R, W, C)


HBM = pl.BlockSpec(memory_space=pltpu.HBM)
VM = pl.BlockSpec(memory_space=pltpu.VMEM)
SM = pl.BlockSpec(memory_space=pltpu.SMEM)
PAY = A + LANES


def params(mib):
    return pltpu.CompilerParams(vmem_limit_bytes=mib * 1024 * 1024)


def shards(
    features, tissue, partner, dw_kernel, dw_bias, ln_gain, ln_bias, w_up,
    narrowing_projection_kernel, layer_scale, w_embed, embed_bias, attn_v, attn_u, attn_w,
):
    block = (S, R, W, C)
    strip = (S, R, 8, C)
    masked_shapes = (
        jax.ShapeDtypeStruct(block, BF),
        jax.ShapeDtypeStruct(strip, BF),
        jax.ShapeDtypeStruct((N, LANES), F32),
    )
    masked, edge, flags = pl.pallas_call(
        mask_kernel,
        out_shape=masked_shapes,
        in_specs=[HBM, HBM],
        out_specs=(HBM, HBM, HBM),
        scratch_shapes=[pltpu.VMEM(block, BF), pltpu.VMEM((R, S, W), jnp.int32)]
        + [pltpu.VMEM(x.shape, x.dtype) for x in masked_shapes]
        + [pltpu.SemaphoreType.DMA((2 * S + 3,))],
        compiler_params=params(60),
        name="mask",
    )(features, tissue.transpose(1, 0, 2))
    tile = ("z", "xl")
    count = lax.axis_size(tile)
    nearby = [(i, i ^ 1) for i in range(count)]
    away = [(i, i + 1 if i % 2 else i - 1) for i in range(1, count - 1)]
    every = ("section",) + tile

    def crossed(moves):
        return [(c * count + i, (1 - c) * count + j) for c in range(2) for i, j in moves]

    far = lax.ppermute(masked, tile, away)
    near = lax.ppermute(masked, tile, nearby)
    edge_own = lax.ppermute(edge, "section", [(0, 1), (1, 0)])
    edge_near = lax.ppermute(edge, every, crossed(nearby))
    edge_far = lax.ppermute(edge, every, crossed(away))
    depth = lax.axis_size("z")

    sources = (masked, dw_kernel)
    partial = jax.ShapeDtypeStruct((N, C), F32)
    partial = pl.pallas_call(
        own_kernel,
        out_shape=partial,
        in_specs=[HBM] * len(sources),
        out_specs=HBM,
        scratch_shapes=[pltpu.VMEM(x.shape, x.dtype) for x in sources + (partial,)]
        + [
            pltpu.VMEM((S, 3 * R, PW, C), F32),
            pltpu.VMEM((R, 7, PW, LANES), F32),
            pltpu.SemaphoreType.DMA((3,)),
        ],
        compiler_params=params(64),
        cost_estimate=pl.CostEstimate(flops=10**8, bytes_accessed=2 * 10**6, transcendentals=0),
        name="own_rows",
    )(*sources)
    operands = (
        edge_own, near, edge_near, far, edge_far, dw_kernel, partial, masked, flags, dw_bias, ln_gain,
        ln_bias, layer_scale, embed_bias, attn_w, w_up, narrowing_projection_kernel, w_embed, attn_v, attn_u,
    )
    forward_shapes = (
        jax.ShapeDtypeStruct((depth, S, PAY), F32),
        jax.ShapeDtypeStruct((N, A), BF),
        jax.ShapeDtypeStruct((N, A), BF),
        jax.ShapeDtypeStruct((N, LANES), F32),
        jax.ShapeDtypeStruct((N, AH), BF),
        jax.ShapeDtypeStruct((N, AH), BF),
    )
    payload, embedded, slope, weight, gate_v, gate_u = pl.pallas_call(
        forward_kernel,
        out_shape=forward_shapes,
        in_specs=[HBM] * len(operands),
        out_specs=[HBM] * len(forward_shapes),
        scratch_shapes=[pltpu.VMEM(x.shape, x.dtype) for x in operands + forward_shapes]
        + [
            pltpu.VMEM((S, 3 * R, PW, C), F32),
            pltpu.VMEM((R, 7, PW, LANES), F32),
            pltpu.VMEM((N, C), F32),
            pltpu.VMEM((S, PAY), F32),
            pltpu.SemaphoreType.DMA((28,)),
        ],
        compiler_params=params(60),
        cost_estimate=pl.CostEstimate(flops=2 * 10**9, bytes_accessed=8 * 10**6, transcendentals=10**6),
        name="forward",
    )(*operands)
    gate_term = pl.pallas_call(
        slope_kernel,
        out_shape=jax.ShapeDtypeStruct((N, C), F32),
        in_specs=[VM] * 3 + [HBM] * 3,
        out_specs=VM,
        scratch_shapes=[
            pltpu.VMEM((C, A), BF),
            pltpu.VMEM((A, AH), BF),
            pltpu.VMEM((A, AH), BF),
            pltpu.SemaphoreType.DMA((3,)),
        ],
        compiler_params=params(24),
        cost_estimate=pl.CostEstimate(flops=10**9, bytes_accessed=4 * 10**6, transcendentals=0),
        name="gate_term",
    )(gate_v, gate_u, slope, w_embed, attn_v, attn_u)

    plane = ("section", "xl", "set")
    received = lax.all_to_all(payload, "z", 0, 0, tiled=True)
    payload = pl.pallas_call(
        sum_kernel,
        out_shape=jax.ShapeDtypeStruct((lax.axis_size(plane), S, PAY), F32),
        in_specs=[VM, HBM],
        out_specs=VM,
        compiler_params=params(24),
        name="add_up",
    )(received, gate_term)
    received = lax.all_to_all(payload, plane, 0, 0, tiled=True)
    slides = partner.shape[0]
    return pl.pallas_call(
        final_kernel,
        out_shape=(
            jax.ShapeDtypeStruct((S,), F32),
            jax.ShapeDtypeStruct((S, A), F32),
            jax.ShapeDtypeStruct((S, R, W, C), BF),
        ),
        in_specs=[VM] * 6 + [HBM],
        out_specs=(SM, VM, VM),
        scratch_shapes=[
            pltpu.VMEM((slides, PAY), F32),
            pltpu.VMEM((C, A), BF),
            pltpu.SemaphoreType.DMA(()),
        ],
        compiler_params=params(24),
        name="final",
    )(received, partner.reshape(1, slides), embedded, slope, weight, gate_term, w_embed)


def solution(mesh):
    section, tile, groups = mesh.devices.shape
    fine = Mesh(
        mesh.devices.reshape(section, tile // 2, 2, groups), ("section", "z", "xl", "set")
    )
    tiles = ("z", "xl")
    placed = (P("set", tiles, "section", None), P("set", tiles, "section")) + (P(),) * 13
    return jax.shard_map(
        shards,
        mesh=fine,
        in_specs=placed,
        out_specs=(P("set"), P("set", None), P("set", tiles, "section", None)),
        check_vma=False,
    )
```
